512 devices in a mesh: pop: 32 (over y, x_hi, core), tile: 16 (over z, x_lo).
Axes of the slice: x: 4 (x_hi: 2, x_lo: 2; x = x_hi * 2 + x_lo), y: 8, z: 8, core: 2. Of those that a mesh axis runs over, the one named last changes fastest.
Arguments:
- weights: int32 [32, 32], replicated, may hold values from -2 to 3
- terminal: float32 [32, 128, 2048], P('pop', 'tile'), may hold values from -4.5 to 4.5
- density_history: bfloat16 [32, 8, 128, 2048], P('pop', None, 'tile'), may hold values from 0.19921875 to 2
- density_init: float32 [32, 128, 2048], P('pop', 'tile'), may hold values from 0.2 to 2
Outputs:
- values: float32 [32, 8, 128, 2048], P('pop', None, 'tile')
- density_final: float32 [32, 128, 2048], P('pop', 'tile')
The draws below stay inside these ranges and needn't reach their ends.
All inputs are finite; a program needn't handle non-finite values.
Results may differ from the reference program's by a relative error of at most 0.0003.
Values may be sent and summed in bfloat16 or wider, within the bound.
No kernel may reach another device: no remote copies, remote signals or barrier semaphores. Data moves between devices by JAX's collectives and lax.ppermute only.
A program may use at most 64 MiB of HBM per device.

```python
import math
import jax
import jax.numpy as jnp
from jax import lax

COLS = 2048
STEPS = 8
POPS = 32
ROWS = 128


def draw_terminal(key, part):
    slope_key = jax.random.fold_in(key, 11)
    phase_key = jax.random.fold_in(key, 12)
    noise_key = jax.random.fold_in(key, 13)
    period = 12.0
    phase = jax.random.randint(phase_key, (POPS, 1, 1), 0, 12).astype(jnp.float32)
    rows = jnp.arange(ROWS, dtype=jnp.float32)[None, :, None]
    position = jnp.mod(rows + phase, period)
    ramp = jnp.abs(position - 0.5 * period) - 0.25 * period
    slope = jax.random.uniform(slope_key, (POPS, 1, 1), jnp.float32, 1.0, 1.25)
    noise = 0.2 * jnp.clip(jax.random.normal(noise_key, (POPS, ROWS, COLS), jnp.float32), -3.0, 3.0)
    return slope * ramp + noise


def set_ends(values, own_key, least, largest):
    extent = values.shape
    place = [jax.random.randint(jax.random.fold_in(own_key, axis), (), 0, extent[axis]) for axis in range(len(extent))]
    values = values.at[tuple(place)].set(least)
    longest = extent.index(max(extent))
    place[longest] = (place[longest] + 1) % extent[longest]
    return values.at[tuple(place)].set(largest)


def level_of(key, shape, cuts, least, high):
    loudness = 1.0
    for dim, parts in cuts:
        draws = jax.random.uniform(jax.random.fold_in(jax.random.fold_in(key, 6), dim), (parts,), jnp.float32, least / len(cuts), high / len(cuts))
        loudness = loudness * jnp.repeat(jnp.exp(draws), shape[dim] // parts).reshape((-1,) + (1,) * (len(shape) - 1 - dim))
    return loudness


def setup_inputs(seed: int = 0) -> dict:
    keys = jax.random.split(jax.random.key(seed), 5)
    weights = set_ends(jax.random.randint(keys[0], (POPS, POPS), -2, 4), jax.random.fold_in(keys[0], 1), -2, 3).astype(jnp.int32)
    terminal = draw_terminal(jax.random.fold_in(keys[4], 71), 0)
    density_history = jnp.clip(jnp.exp(math.log(2.0) - 2.306499 * jax.random.uniform(keys[2], (POPS, STEPS, ROWS, COLS), jnp.float32) ** level_of(keys[2], (POPS, STEPS, ROWS, COLS), ((0, 32), (2, 16)), -0.2, 0.2)), 0.19921875, 2.0).astype(jnp.bfloat16)
    density_init = jnp.clip(jnp.exp(math.log(2.0) - 2.3025851 * jax.random.uniform(keys[3], (POPS, ROWS, COLS), jnp.float32) ** level_of(keys[3], (POPS, ROWS, COLS), ((0, 32), (1, 16)), -0.2, 0.2)), 0.2, 2.0)
    return dict(weights=weights, terminal=terminal, density_history=density_history, density_init=density_init)


time_step = 0.2
viscosity = 0.2


def laplace(field):
    return jnp.roll(field, -1, 1) + jnp.roll(field, 1, 1) + jnp.roll(field, -1, 2) + jnp.roll(field, 1, 2) - 4.0 * field


def hamiltonian(field):
    ahead_rows = jnp.minimum(jnp.roll(field, -1, 1) - field, 0.0)
    behind_rows = jnp.maximum(field - jnp.roll(field, 1, 1), 0.0)
    ahead_cols = jnp.minimum(jnp.roll(field, -1, 2) - field, 0.0)
    behind_cols = jnp.maximum(field - jnp.roll(field, 1, 2), 0.0)
    return 0.5 * (behind_rows * behind_rows + ahead_rows * ahead_rows + behind_cols * behind_cols + ahead_cols * ahead_cols)


def transport(density, value):
    drift_rows = -(jnp.roll(value, -1, 1) - value)
    flux_rows = jnp.maximum(drift_rows, 0.0) * density + jnp.minimum(drift_rows, 0.0) * jnp.roll(density, -1, 1)
    drift_cols = -(jnp.roll(value, -1, 2) - value)
    flux_cols = jnp.maximum(drift_cols, 0.0) * density + jnp.minimum(drift_cols, 0.0) * jnp.roll(density, -1, 2)
    div_rows = flux_rows - jnp.roll(flux_rows, 1, 1)
    div_cols = flux_cols - jnp.roll(flux_cols, 1, 2)
    return density + time_step * (viscosity * laplace(density) - div_rows - div_cols)


def reference(weights, terminal, density_history, density_init):
    factors = weights.astype(jnp.float32)
    current = terminal
    centred = [None] * STEPS
    for step in reversed(range(STEPS)):
        coupled = jnp.einsum("pq,qrc->prc", factors, density_history[:, step].astype(jnp.float32), precision=lax.Precision.HIGHEST) / POPS
        advanced = current + time_step * (viscosity * laplace(current) - hamiltonian(current) + coupled)
        advanced = advanced - jnp.mean(advanced, axis=(1, 2), keepdims=True)
        centred[step] = advanced
        current = advanced
    density = density_init
    for step in range(STEPS):
        density = transport(density, centred[step])
    return jnp.stack(centred, axis=1), density
```

```python
import functools

import jax
import jax.numpy as jnp
from jax import lax
from jax.experimental import pallas as pl
from jax.experimental.pallas import tpu as pltpu
from jax.sharding import Mesh
from jax.sharding import PartitionSpec as P

POP = ("pop_0", "pop_1", "pop_2")

time_step = 0.2
viscosity = 0.2

DENSITY_MID = (0.19921875 + 2.0) / 2
DENSITY_HALF = (2.0 - 0.19921875) / 2
LEVELS = 32000.0
TERMINAL_SCALE = 32000.0 / 4.5

HALO = 8
F32 = jnp.float32
I16 = jnp.int16


def to_i16(x):
    return jnp.round(x).astype(jnp.int32).astype(I16)


def coupling_kernel(w_ref, x_ref, out_ref):
    pops = w_ref.shape[0]
    rows = x_ref.shape[0]
    per = rows // pops
    shift = per.bit_length() - 1
    weights = w_ref[...].astype(F32).astype(jnp.bfloat16)
    i = lax.broadcasted_iota(jnp.int32, (rows, pops), 0)
    q = lax.broadcasted_iota(jnp.int32, (rows, pops), 1)
    spread = jnp.where((i >> shift) == q, 1.0, 0.0).astype(jnp.bfloat16)
    tall = jnp.dot(spread, weights, preferred_element_type=F32)
    total = jnp.sum(tall, axis=1, keepdims=True)
    size = jnp.maximum(jnp.sum(jnp.abs(tall), axis=1, keepdims=True), 1.0)
    wide = lax.dot_general(
        tall.astype(jnp.bfloat16), spread, (((1,), (1,)), ((), ())), preferred_element_type=F32
    )
    a = lax.broadcasted_iota(jnp.int32, (rows, rows), 0)
    b = lax.broadcasted_iota(jnp.int32, (rows, rows), 1)
    kron = jnp.where((a & (per - 1)) == (b & (per - 1)), wide, 0.0).astype(jnp.bfloat16)
    product = jnp.dot(kron, x_ref[...], preferred_element_type=F32)
    level = (product - DENSITY_MID * total) * (LEVELS / (DENSITY_HALF * size))
    out_ref[...] = to_i16(level)


def rows_of_step(wide, step, blocks):
    first = step * blocks * HALO
    return jnp.concatenate(
        [wide[first + k * HALO : first + (k + 1) * HALO] for k in range(blocks)], axis=1
    )


def pack_kernel(blocks, steps, c_ref, terminal_ref, down_ref, up_ref):
    wide = c_ref[...].astype(F32)
    c = [rows_of_step(wide, t, blocks) for t in range(steps)]
    row = lax.broadcasted_iota(jnp.int32, c[0].shape, 0)
    down = []
    up = []
    for t in range(1, HALO // 2):
        down.append(jnp.where(row >= t, c[HALO - t], pltpu.roll(c[t], t, 0)))
        up.append(jnp.where(row < HALO - t, c[HALO - t], pltpu.roll(c[t], HALO - t, 0)))
    down.append(c[HALO // 2])
    up.append(c[HALO // 2])
    edge = terminal_ref[...] * TERMINAL_SCALE
    down_ref[...] = to_i16(jnp.concatenate(down + [edge], axis=0))
    up_ref[...] = to_i16(jnp.concatenate(up + [edge], axis=0))


def backward_kernel(
    blocks, steps, w_ref, c_ref, terminal_ref, init_ref, above_ref, below_ref, u_ref, edge_ref, sums_ref
):
    pops = w_ref.shape[0]
    cols = terminal_ref.shape[1]
    own = lax.axis_index(POP)
    own_weights = w_ref[pl.ds(own, 1), :].astype(F32)
    total = jnp.sum(own_weights, axis=1, keepdims=True)
    size = jnp.maximum(jnp.sum(jnp.abs(own_weights), axis=1, keepdims=True), 1.0)
    slope = size * (DENSITY_HALF / (LEVELS * pops))
    offset = total * (DENSITY_MID / pops)
    wide = c_ref[...].astype(F32)
    above = above_ref[...].astype(F32)
    below = below_ref[...].astype(F32)

    def tile(x, k):
        return x[k * HALO : (k + 1) * HALO]

    def levels(t):
        if t == 0:
            top = bottom = jnp.zeros((HALO, cols), F32)
        elif t <= HALO // 2:
            top = tile(above, t - 1)
            bottom = tile(below, t - 1)
            if t < HALO // 2:
                top = pltpu.roll(top, HALO - t, 0)
                bottom = pltpu.roll(bottom, t, 0)
        else:
            top = tile(above, HALO - t - 1)
            bottom = tile(below, HALO - t - 1)
        return jnp.concatenate([top, rows_of_step(wide, t, blocks), bottom], axis=0)

    last = HALO // 2
    u = jnp.concatenate(
        [
            tile(above, last) * (1.0 / TERMINAL_SCALE),
            terminal_ref[...],
            tile(below, last) * (1.0 / TERMINAL_SCALE),
        ],
        axis=0,
    )
    high = u.shape[0]
    partial = [None] * steps
    kept = [None] * steps
    for t in reversed(range(steps)):
        coupled = levels(t) * slope + offset
        behind_r = u - pltpu.roll(u, 1, 0)
        ahead_r = pltpu.roll(u, high - 1, 0) - u
        behind_c = u - pltpu.roll(u, 1, 1)
        ahead_c = pltpu.roll(u, cols - 1, 1) - u
        lap = (ahead_r - behind_r) + (ahead_c - behind_c)
        br = jnp.maximum(behind_r, 0.0)
        ar = jnp.minimum(ahead_r, 0.0)
        bc = jnp.maximum(behind_c, 0.0)
        ac = jnp.minimum(ahead_c, 0.0)
        ham = 0.5 * (br * br + ar * ar + bc * bc + ac * ac)
        u = u + time_step * (viscosity * lap - ham + coupled)
        u_ref[t] = u
        mine = u[HALO : 2 * HALO]
        kept[t] = mine
        lanes = mine[:, :128]
        for k in range(1, cols // 128):
            lanes = lanes + mine[:, k * 128 : (k + 1) * 128]
        partial[t] = jnp.sum(lanes, axis=0, keepdims=True)
    sums = jnp.concatenate(partial, axis=0)
    sums_ref[...] = jnp.broadcast_to(sums[None], sums_ref.shape)
    row = lax.broadcasted_iota(jnp.int32, (HALO, cols), 0)
    edge_ref[0:8] = init_ref[...]
    edge_ref[8:16] = kept[0]
    edge_ref[16:24] = jnp.where((row >= 1) & (row <= 6), kept[1], pltpu.roll(kept[3], 4, 0))
    edge_ref[24:32] = kept[2]


def forward_kernel(
    cells, steps, u_ref, init_ref, above_ref, below_ref, sums_ref, values_ref, final_ref
):
    cols = init_ref.shape[1]
    means = jnp.sum(jnp.sum(sums_ref[...], axis=0), axis=1, keepdims=True) * (1.0 / cells)
    row = lax.broadcasted_iota(jnp.int32, (HALO, cols), 0)
    m = jnp.concatenate([above_ref[0:8], init_ref[...], below_ref[0:8]], axis=0)
    high = m.shape[0]

    def field(t):
        u = u_ref[t]
        if t > 3:
            return u

        def side(ref, near):
            if t == 0:
                return ref[8:16]
            if t == 1:
                return jnp.where((row >= 1) & (row <= 6), ref[16:24], near)
            if t == 2:
                return jnp.where((row >= 2) & (row <= 5), ref[24:32], near)
            return jnp.where((row >= 3) & (row <= 4), pltpu.roll(ref[16:24], 4, 0), near)

        return jnp.concatenate(
            [side(above_ref, u[0:8]), u[8:16], side(below_ref, u[16:24])], axis=0
        )

    for t in range(steps):
        values_ref[t] = u_ref[t, HALO : 2 * HALO, :] - means[t : t + 1, :]
        u = field(t)
        down_m = pltpu.roll(m, high - 1, 0)
        right_m = pltpu.roll(m, cols - 1, 1)
        drift_r = u - pltpu.roll(u, high - 1, 0)
        drift_c = u - pltpu.roll(u, cols - 1, 1)
        flux_r = (
            jnp.maximum(drift_r, 0.0) * m
            + jnp.minimum(drift_r, 0.0) * down_m
            - viscosity * (down_m - m)
        )
        flux_c = (
            jnp.maximum(drift_c, 0.0) * m
            + jnp.minimum(drift_c, 0.0) * right_m
            - viscosity * (right_m - m)
        )
        m = m - time_step * (
            (flux_r - pltpu.roll(flux_r, 1, 0)) + (flux_c - pltpu.roll(flux_c, 1, 1))
        )
    final_ref[...] = m[HALO : 2 * HALO]


def call(kernel, outs, *args):
    spec = pl.BlockSpec(memory_space=pltpu.VMEM)
    return pl.pallas_call(
        kernel,
        out_shape=outs,
        in_specs=[spec] * len(args),
        out_specs=jax.tree.map(lambda _: spec, outs),
        compiler_params=pltpu.CompilerParams(vmem_limit_bytes=40 * 1024 * 1024),
    )(*args)


def shifted(x, by):
    peers = lax.axis_size("tile")
    return lax.ppermute(x, "tile", [(i, (i + by) % peers) for i in range(peers)])


def per_device(weights, terminal, density_history, density_init):
    pops = weights.shape[0]
    steps, rows, cols = density_history.shape[1:]
    tiles = lax.axis_size("tile")
    blocks = pops // steps
    part = cols // blocks
    struct = jax.ShapeDtypeStruct
    terminal = terminal[0]
    init = density_init[0]
    chunks = density_history[0].reshape(steps, rows, blocks, part).transpose(0, 2, 1, 3)
    chunks = lax.all_to_all(chunks.reshape(pops, rows, part), POP, 0, 0, tiled=True)
    levels = call(
        coupling_kernel, struct((pops * rows, part), I16), weights, chunks.reshape(pops * rows, part)
    )
    levels = lax.all_to_all(levels.reshape(pops, rows, part), POP, 0, 0, tiled=True)
    levels = levels.reshape(pops * rows, part)
    down, up = call(
        functools.partial(pack_kernel, blocks, steps),
        (struct((40, cols), I16), struct((40, cols), I16)),
        levels,
        terminal,
    )
    above = shifted(down, 1)
    below = shifted(up, -1)
    fields, edges, sums = call(
        functools.partial(backward_kernel, blocks, steps),
        (
            struct((steps, 3 * HALO, cols), F32),
            struct((32, cols), F32),
            struct((tiles, steps, 128), F32),
        ),
        weights,
        levels,
        terminal,
        init,
        above,
        below,
    )
    above = shifted(edges, 1)
    below = shifted(edges, -1)
    sums = lax.all_to_all(sums, "tile", 0, 0, tiled=True)
    values, final = call(
        functools.partial(forward_kernel, float(tiles * rows * cols), steps),
        (struct((steps, rows, cols), F32), struct((rows, cols), F32)),
        fields,
        init,
        above,
        below,
        sums,
    )
    return values[None], final[None]


def solution(mesh):
    split = Mesh(
        mesh.devices.reshape(8, 2, 2, mesh.shape["tile"]), ("pop_0", "pop_1", "pop_2", "tile")
    )
    in_specs = (P(), P(POP, "tile", None), P(POP, None, "tile", None), P(POP, "tile", None))
    out_specs = (P(POP, None, "tile", None), P(POP, "tile", None))
    return jax.shard_map(
        per_device, mesh=split, in_specs=in_specs, out_specs=out_specs, check_vma=False
    )
```

```python
import functools

import jax
import jax.numpy as jnp
from jax import lax
from jax.experimental import pallas as pl
from jax.experimental.pallas import tpu as pltpu
from jax.sharding import Mesh
from jax.sharding import PartitionSpec as P

POP = ("pop_0", "pop_1", "pop_2")

time_step = 0.2
viscosity = 0.2

DENSITY_MID = (0.19921875 + 2.0) / 2
DENSITY_HALF = (2.0 - 0.19921875) / 2
LEVELS = 32000.0
TERMINAL_SCALE = 32000.0 / 4.5

HALO = 8
F32 = jnp.float32
I16 = jnp.int16


def to_i16(x):
    return jnp.round(x).astype(jnp.int32).astype(I16)


def coupling_kernel(w_ref, x_ref, out_ref):
    pops = w_ref.shape[0]
    rows = x_ref.shape[0]
    per = rows // pops
    shift = per.bit_length() - 1
    weights = w_ref[...].astype(F32).astype(jnp.bfloat16)
    i = lax.broadcasted_iota(jnp.int32, (rows, pops), 0)
    q = lax.broadcasted_iota(jnp.int32, (rows, pops), 1)
    spread = jnp.where((i >> shift) == q, 1.0, 0.0).astype(jnp.bfloat16)
    tall = jnp.dot(spread, weights, preferred_element_type=F32)
    total = jnp.sum(tall, axis=1, keepdims=True)
    size = jnp.maximum(jnp.sum(jnp.abs(tall), axis=1, keepdims=True), 1.0)
    wide = lax.dot_general(
        tall.astype(jnp.bfloat16), spread, (((1,), (1,)), ((), ())), preferred_element_type=F32
    )
    a = lax.broadcasted_iota(jnp.int32, (rows, rows), 0)
    b = lax.broadcasted_iota(jnp.int32, (rows, rows), 1)
    kron = jnp.where((a & (per - 1)) == (b & (per - 1)), wide, 0.0).astype(jnp.bfloat16)
    product = jnp.dot(kron, x_ref[...], preferred_element_type=F32)
    level = (product - DENSITY_MID * total) * (LEVELS / (DENSITY_HALF * size))
    out_ref[...] = to_i16(level)


def rows_of_step(wide, step, blocks):
    first = step * blocks * HALO
    return jnp.concatenate(
        [wide[first + k * HALO : first + (k + 1) * HALO] for k in range(blocks)], axis=1
    )


def is_even():
    return (lax.axis_index("tile") & 1) == 0


def pack_kernel(blocks, steps, c_ref, terminal_ref, first_ref, second_ref):
    wide = c_ref[...].astype(F32)
    c = [rows_of_step(wide, t, blocks) for t in range(steps)]
    row = lax.broadcasted_iota(jnp.int32, c[0].shape, 0)
    down = []
    up = []
    for t in range(1, HALO // 2):
        down.append(jnp.where(row >= t, c[HALO - t], pltpu.roll(c[t], t, 0)))
        up.append(jnp.where(row < HALO - t, c[HALO - t], pltpu.roll(c[t], HALO - t, 0)))
    even = is_even()
    edge = terminal_ref[...] * TERMINAL_SCALE
    first = [jnp.where(even, d, u) for d, u in zip(down, up)] + [c[HALO // 2], edge]
    second = [jnp.where(even, u, d) for d, u in zip(down, up)] + [c[HALO // 2], edge]
    first_ref[...] = to_i16(jnp.concatenate(first, axis=0))
    second_ref[...] = to_i16(jnp.concatenate(second, axis=0))


def backward_kernel(
    blocks, steps, w_ref, c_ref, terminal_ref, init_ref, first_ref, second_ref, u_ref, edge_ref, sums_ref
):
    pops = w_ref.shape[0]
    cols = terminal_ref.shape[1]
    own = lax.axis_index(POP)
    own_weights = w_ref[pl.ds(own, 1), :].astype(F32)
    total = jnp.sum(own_weights, axis=1, keepdims=True)
    size = jnp.maximum(jnp.sum(jnp.abs(own_weights), axis=1, keepdims=True), 1.0)
    slope = size * (DENSITY_HALF / (LEVELS * pops))
    offset = total * (DENSITY_MID / pops)
    wide = c_ref[...].astype(F32)
    even = is_even()
    first = first_ref[...].astype(F32)
    second = second_ref[...].astype(F32)
    above = jnp.where(even, second, first)
    below = jnp.where(even, first, second)

    def tile(x, k):
        return x[k * HALO : (k + 1) * HALO]

    def levels(t):
        if t == 0:
            top = bottom = jnp.zeros((HALO, cols), F32)
        elif t <= HALO // 2:
            top = tile(above, t - 1)
            bottom = tile(below, t - 1)
            if t < HALO // 2:
                top = pltpu.roll(top, HALO - t, 0)
                bottom = pltpu.roll(bottom, t, 0)
        else:
            top = tile(above, HALO - t - 1)
            bottom = tile(below, HALO - t - 1)
        return jnp.concatenate([top, rows_of_step(wide, t, blocks), bottom], axis=0)

    last = HALO // 2
    u = jnp.concatenate(
        [
            tile(above, last) * (1.0 / TERMINAL_SCALE),
            terminal_ref[...],
            tile(below, last) * (1.0 / TERMINAL_SCALE),
        ],
        axis=0,
    )
    high = u.shape[0]
    partial = [None] * steps
    kept = [None] * steps
    for t in reversed(range(steps)):
        coupled = levels(t) * slope + offset
        behind_r = u - pltpu.roll(u, 1, 0)
        ahead_r = pltpu.roll(u, high - 1, 0) - u
        behind_c = u - pltpu.roll(u, 1, 1)
        ahead_c = pltpu.roll(u, cols - 1, 1) - u
        lap = (ahead_r - behind_r) + (ahead_c - behind_c)
        br = jnp.maximum(behind_r, 0.0)
        ar = jnp.minimum(ahead_r, 0.0)
        bc = jnp.maximum(behind_c, 0.0)
        ac = jnp.minimum(ahead_c, 0.0)
        ham = 0.5 * (br * br + ar * ar + bc * bc + ac * ac)
        u = u + time_step * (viscosity * lap - ham + coupled)
        u_ref[t] = u
        mine = u[HALO : 2 * HALO]
        kept[t] = mine
        lanes = mine[:, :128]
        for k in range(1, cols // 128):
            lanes = lanes + mine[:, k * 128 : (k + 1) * 128]
        partial[t] = jnp.sum(lanes, axis=0, keepdims=True)
    sums = jnp.sum(jnp.concatenate(partial, axis=0), axis=1, keepdims=True)
    lane = lax.broadcasted_iota(jnp.int32, (steps, 128), 1)
    step = lax.broadcasted_iota(jnp.int32, (steps, 128), 0)
    line = jnp.sum(jnp.where(lane == step, sums, 0.0), axis=0, keepdims=True)
    sums_ref[...] = jnp.broadcast_to(line[None], sums_ref.shape)
    row = lax.broadcasted_iota(jnp.int32, (HALO, cols), 0)
    edge_ref[0:8] = init_ref[...]
    edge_ref[8:16] = kept[0]
    edge_ref[16:24] = jnp.where((row >= 1) & (row <= 6), kept[1], pltpu.roll(kept[3], 4, 0))
    edge_ref[24:32] = kept[2]


def forward_kernel(
    cells, steps, u_ref, init_ref, second_ref, first_ref, sums_ref, values_ref, final_ref
):
    cols = init_ref.shape[1]
    means = jnp.sum(sums_ref[...], axis=0) * (1.0 / cells)
    row = lax.broadcasted_iota(jnp.int32, (HALO, cols), 0)
    even = is_even()
    first = first_ref[...]
    second = second_ref[...]
    above = jnp.where(even, second, first)
    below = jnp.where(even, first, second)
    m = jnp.concatenate([above[0:8], init_ref[...], below[0:8]], axis=0)
    high = m.shape[0]

    def field(t):
        u = u_ref[t]
        if t > 3:
            return u

        def side(far, near):
            if t == 0:
                return far[8:16]
            if t == 1:
                return jnp.where((row >= 1) & (row <= 6), far[16:24], near)
            if t == 2:
                return jnp.where((row >= 2) & (row <= 5), far[24:32], near)
            return jnp.where((row >= 3) & (row <= 4), pltpu.roll(far[16:24], 4, 0), near)

        return jnp.concatenate(
            [side(above, u[0:8]), u[8:16], side(below, u[16:24])], axis=0
        )

    for t in range(steps):
        values_ref[t] = u_ref[t, HALO : 2 * HALO, :] - means[:, t : t + 1]
        u = field(t)
        down_m = pltpu.roll(m, high - 1, 0)
        right_m = pltpu.roll(m, cols - 1, 1)
        drift_r = u - pltpu.roll(u, high - 1, 0)
        drift_c = u - pltpu.roll(u, cols - 1, 1)
        flux_r = (
            jnp.maximum(drift_r, 0.0) * m
            + jnp.minimum(drift_r, 0.0) * down_m
            - viscosity * (down_m - m)
        )
        flux_c = (
            jnp.maximum(drift_c, 0.0) * m
            + jnp.minimum(drift_c, 0.0) * right_m
            - viscosity * (right_m - m)
        )
        m = m - time_step * (
            (flux_r - pltpu.roll(flux_r, 1, 0)) + (flux_c - pltpu.roll(flux_c, 1, 1))
        )
    final_ref[...] = m[HALO : 2 * HALO]


def call(kernel, outs, *args):
    spec = pl.BlockSpec(memory_space=pltpu.VMEM)
    return pl.pallas_call(
        kernel,
        out_shape=outs,
        in_specs=[spec] * len(args),
        out_specs=jax.tree.map(lambda _: spec, outs),
        compiler_params=pltpu.CompilerParams(vmem_limit_bytes=40 * 1024 * 1024),
    )(*args)


def first_swap(x):
    peers = lax.axis_size("tile")
    return lax.ppermute(x, "tile", [(i, i ^ 1) for i in range(peers)])


def second_swap(x):
    peers = lax.axis_size("tile")
    return lax.ppermute(x, "tile", [(i, (((i + 1) ^ 1) - 1) % peers) for i in range(peers)])


def per_device(weights, terminal, density_history, density_init):
    pops = weights.shape[0]
    steps, rows, cols = density_history.shape[1:]
    tiles = lax.axis_size("tile")
    blocks = pops // steps
    part = cols // blocks
    struct = jax.ShapeDtypeStruct
    terminal = terminal[0]
    init = density_init[0]
    chunks = density_history[0].reshape(steps, rows, blocks, part).transpose(0, 2, 1, 3)
    chunks = lax.all_to_all(chunks.reshape(pops, rows, part), POP, 0, 0, tiled=True)
    levels = call(
        coupling_kernel, struct((pops * rows, part), I16), weights, chunks.reshape(pops * rows, part)
    )
    levels = lax.all_to_all(levels.reshape(pops, rows, part), POP, 0, 0, tiled=True)
    levels = levels.reshape(pops * rows, part)
    first, second = call(
        functools.partial(pack_kernel, blocks, steps),
        (struct((40, cols), I16), struct((40, cols), I16)),
        levels,
        terminal,
    )
    second = second_swap(second)
    first = first_swap(first)
    fields, edges, sums = call(
        functools.partial(backward_kernel, blocks, steps),
        (
            struct((steps, 3 * HALO, cols), F32),
            struct((32, cols), F32),
            struct((tiles, 1, 128), F32),
        ),
        weights,
        levels,
        terminal,
        init,
        first,
        second,
    )
    first = first_swap(edges)
    second = second_swap(edges)
    sums = lax.all_to_all(sums, "tile", 0, 0, tiled=True)
    values, final = call(
        functools.partial(forward_kernel, float(tiles * rows * cols), steps),
        (struct((steps, rows, cols), F32), struct((rows, cols), F32)),
        fields,
        init,
        second,
        first,
        sums,
    )
    return values[None], final[None]


def solution(mesh):
    split = Mesh(
        mesh.devices.reshape(8, 2, 2, mesh.shape["tile"]), ("pop_0", "pop_1", "pop_2", "tile")
    )
    in_specs = (P(), P(POP, "tile", None), P(POP, None, "tile", None), P(POP, "tile", None))
    out_specs = (P(POP, None, "tile", None), P(POP, "tile", None))
    return jax.shard_map(
        per_device, mesh=split, in_specs=in_specs, out_specs=out_specs, check_vma=False
    )
```

```python
import functools

import jax
import jax.numpy as jnp
from jax import lax
from jax.experimental import pallas as pl
from jax.experimental.pallas import tpu as pltpu
from jax.sharding import Mesh
from jax.sharding import PartitionSpec as P

POP = ("pop_0", "pop_1", "pop_2")

time_step = 0.2
viscosity = 0.2

DENSITY_MID = (0.19921875 + 2.0) / 2
DENSITY_HALF = (2.0 - 0.19921875) / 2
LEVELS = 32000.0
TERMINAL_SCALE = 32000.0 / 4.5

HALO = 8
F32 = jnp.float32
I16 = jnp.int16


def to_i16(x):
    return jnp.round(x).astype(jnp.int32).astype(I16)


def spread_kernel(w_ref, kron_ref, scale_ref):
    pops = w_ref.shape[0]
    rows = kron_ref.shape[0]
    per = rows // pops
    shift = per.bit_length() - 1
    weights = w_ref[...].astype(F32).astype(jnp.bfloat16)
    i = lax.broadcasted_iota(jnp.int32, (rows, pops), 0)
    q = lax.broadcasted_iota(jnp.int32, (rows, pops), 1)
    spread = jnp.where((i >> shift) == q, 1.0, 0.0).astype(jnp.bfloat16)
    tall = jnp.dot(spread, weights, preferred_element_type=F32)
    total = jnp.sum(tall, axis=1, keepdims=True)
    size = jnp.maximum(jnp.sum(jnp.abs(tall), axis=1, keepdims=True), 1.0)
    wide = lax.dot_general(
        tall.astype(jnp.bfloat16), spread, (((1,), (1,)), ((), ())), preferred_element_type=F32
    )
    a = lax.broadcasted_iota(jnp.int32, (rows, rows), 0)
    b = lax.broadcasted_iota(jnp.int32, (rows, rows), 1)
    kron_ref[...] = jnp.where((a & (per - 1)) == (b & (per - 1)), wide, 0.0).astype(jnp.bfloat16)
    lane = lax.broadcasted_iota(jnp.int32, scale_ref.shape, 1)
    scale_ref[...] = jnp.where(
        lane == 0, DENSITY_MID * total, LEVELS / (DENSITY_HALF * size)
    )


def coupling_kernel(kron_ref, scale_ref, x_ref, out_ref):
    product = jnp.dot(kron_ref[...], x_ref[...], preferred_element_type=F32)
    out_ref[...] = to_i16((product - scale_ref[:, 0:1]) * scale_ref[:, 1:2])


def rows_of_step(wide, step, blocks):
    first = step * blocks * HALO
    return jnp.concatenate(
        [wide[first + k * HALO : first + (k + 1) * HALO] for k in range(blocks)], axis=1
    )


def is_even():
    return (lax.axis_index("tile") & 1) == 0


def pack_kernel(blocks, steps, c_ref, terminal_ref, first_ref, second_ref):
    wide = c_ref[...].astype(F32)
    c = [rows_of_step(wide, t, blocks) for t in range(steps)]
    row = lax.broadcasted_iota(jnp.int32, c[0].shape, 0)
    down = []
    up = []
    for t in range(1, HALO // 2):
        down.append(jnp.where(row >= t, c[HALO - t], pltpu.roll(c[t], t, 0)))
        up.append(jnp.where(row < HALO - t, c[HALO - t], pltpu.roll(c[t], HALO - t, 0)))
    even = is_even()
    edge = terminal_ref[...] * TERMINAL_SCALE
    first = [jnp.where(even, d, u) for d, u in zip(down, up)] + [c[HALO // 2], edge]
    second = [jnp.where(even, u, d) for d, u in zip(down, up)] + [c[HALO // 2], edge]
    first_ref[...] = to_i16(jnp.concatenate(first, axis=0))
    second_ref[...] = to_i16(jnp.concatenate(second, axis=0))


def backward_kernel(
    blocks, steps, w_ref, c_ref, terminal_ref, init_ref, first_ref, second_ref, u_ref, edge_ref, sums_ref
):
    pops = w_ref.shape[0]
    cols = terminal_ref.shape[1]
    own = lax.axis_index(POP)
    own_weights = w_ref[pl.ds(own, 1), :].astype(F32)
    total = jnp.sum(own_weights, axis=1, keepdims=True)
    size = jnp.maximum(jnp.sum(jnp.abs(own_weights), axis=1, keepdims=True), 1.0)
    slope = size * (DENSITY_HALF / (LEVELS * pops))
    offset = total * (DENSITY_MID / pops)
    wide = c_ref[...].astype(F32)
    even = is_even()
    first = first_ref[...].astype(F32)
    second = second_ref[...].astype(F32)
    above = jnp.where(even, second, first)
    below = jnp.where(even, first, second)

    def tile(x, k):
        return x[k * HALO : (k + 1) * HALO]

    def levels(t):
        if t == 0:
            top = bottom = jnp.zeros((HALO, cols), F32)
        elif t <= HALO // 2:
            top = tile(above, t - 1)
            bottom = tile(below, t - 1)
            if t < HALO // 2:
                top = pltpu.roll(top, HALO - t, 0)
                bottom = pltpu.roll(bottom, t, 0)
        else:
            top = tile(above, HALO - t - 1)
            bottom = tile(below, HALO - t - 1)
        return jnp.concatenate([top, rows_of_step(wide, t, blocks), bottom], axis=0)

    last = HALO // 2
    u = jnp.concatenate(
        [
            tile(above, last) * (1.0 / TERMINAL_SCALE),
            terminal_ref[...],
            tile(below, last) * (1.0 / TERMINAL_SCALE),
        ],
        axis=0,
    )
    high = u.shape[0]
    partial = [None] * steps
    kept = [None] * steps
    for t in reversed(range(steps)):
        coupled = levels(t) * slope + offset
        behind_r = u - pltpu.roll(u, 1, 0)
        ahead_r = pltpu.roll(u, high - 1, 0) - u
        behind_c = u - pltpu.roll(u, 1, 1)
        ahead_c = pltpu.roll(u, cols - 1, 1) - u
        lap = (ahead_r - behind_r) + (ahead_c - behind_c)
        br = jnp.maximum(behind_r, 0.0)
        ar = jnp.minimum(ahead_r, 0.0)
        bc = jnp.maximum(behind_c, 0.0)
        ac = jnp.minimum(ahead_c, 0.0)
        ham = 0.5 * (br * br + ar * ar + bc * bc + ac * ac)
        u = u + time_step * (viscosity * lap - ham + coupled)
        u_ref[t] = u
        mine = u[HALO : 2 * HALO]
        kept[t] = mine
        lanes = mine[:, :128]
        for k in range(1, cols // 128):
            lanes = lanes + mine[:, k * 128 : (k + 1) * 128]
        partial[t] = jnp.sum(lanes, axis=0, keepdims=True)
    sums = jnp.sum(jnp.concatenate(partial, axis=0), axis=1, keepdims=True)
    lane = lax.broadcasted_iota(jnp.int32, (steps, 128), 1)
    step = lax.broadcasted_iota(jnp.int32, (steps, 128), 0)
    line = jnp.sum(jnp.where(lane == step, sums, 0.0), axis=0, keepdims=True)
    sums_ref[...] = jnp.broadcast_to(line[None], sums_ref.shape)
    row = lax.broadcasted_iota(jnp.int32, (HALO, cols), 0)
    edge_ref[0:8] = init_ref[...]
    edge_ref[8:16] = kept[0]
    edge_ref[16:24] = jnp.where((row >= 1) & (row <= 6), kept[1], pltpu.roll(kept[3], 4, 0))
    edge_ref[24:32] = kept[2]


def forward_kernel(
    steps, u_ref, init_ref, second_ref, first_ref, final_ref
):
    cols = init_ref.shape[1]
    row = lax.broadcasted_iota(jnp.int32, (HALO, cols), 0)
    even = is_even()
    first = first_ref[...]
    second = second_ref[...]
    above = jnp.where(even, second, first)
    below = jnp.where(even, first, second)
    m = jnp.concatenate([above[0:8], init_ref[...], below[0:8]], axis=0)
    high = m.shape[0]

    def field(t):
        u = u_ref[t]
        if t > 3:
            return u

        def side(far, near):
            if t == 0:
                return far[8:16]
            if t == 1:
                return jnp.where((row >= 1) & (row <= 6), far[16:24], near)
            if t == 2:
                return jnp.where((row >= 2) & (row <= 5), far[24:32], near)
            return jnp.where((row >= 3) & (row <= 4), pltpu.roll(far[16:24], 4, 0), near)

        return jnp.concatenate(
            [side(above, u[0:8]), u[8:16], side(below, u[16:24])], axis=0
        )

    for t in range(steps):
        u = field(t)
        down_m = pltpu.roll(m, high - 1, 0)
        right_m = pltpu.roll(m, cols - 1, 1)
        drift_r = u - pltpu.roll(u, high - 1, 0)
        drift_c = u - pltpu.roll(u, cols - 1, 1)
        flux_r = (
            jnp.maximum(drift_r, 0.0) * m
            + jnp.minimum(drift_r, 0.0) * down_m
            - viscosity * (down_m - m)
        )
        flux_c = (
            jnp.maximum(drift_c, 0.0) * m
            + jnp.minimum(drift_c, 0.0) * right_m
            - viscosity * (right_m - m)
        )
        m = m - time_step * (
            (flux_r - pltpu.roll(flux_r, 1, 0)) + (flux_c - pltpu.roll(flux_c, 1, 1))
        )
    final_ref[...] = m[HALO : 2 * HALO]


def centre_kernel(cells, steps, u_ref, sums_ref, values_ref):
    means = jnp.sum(sums_ref[...], axis=0) * (1.0 / cells)
    for t in range(steps):
        values_ref[t] = u_ref[t, HALO : 2 * HALO, :] - means[:, t : t + 1]


def call(kernel, outs, *args):
    spec = pl.BlockSpec(memory_space=pltpu.VMEM)
    return pl.pallas_call(
        kernel,
        out_shape=outs,
        in_specs=[spec] * len(args),
        out_specs=jax.tree.map(lambda _: spec, outs),
        compiler_params=pltpu.CompilerParams(vmem_limit_bytes=40 * 1024 * 1024),
    )(*args)


def first_swap(x):
    peers = lax.axis_size("tile")
    return lax.ppermute(x, "tile", [(i, i ^ 1) for i in range(peers)])


def second_swap(x):
    peers = lax.axis_size("tile")
    return lax.ppermute(x, "tile", [(i, (((i + 1) ^ 1) - 1) % peers) for i in range(peers)])


def per_device(weights, terminal, density_history, density_init):
    pops = weights.shape[0]
    steps, rows, cols = density_history.shape[1:]
    tiles = lax.axis_size("tile")
    blocks = pops // steps
    part = cols // blocks
    struct = jax.ShapeDtypeStruct
    terminal = terminal[0]
    init = density_init[0]
    chunks = density_history[0].reshape(steps, rows, blocks, part).transpose(0, 2, 1, 3)
    chunks = lax.all_to_all(chunks.reshape(pops, rows, part), POP, 0, 0, tiled=True)
    kron, scale = call(
        spread_kernel,
        (struct((pops * rows, pops * rows), jnp.bfloat16), struct((pops * rows, 128), F32)),
        weights,
    )
    levels = call(
        coupling_kernel,
        struct((pops * rows, part), I16),
        kron,
        scale,
        chunks.reshape(pops * rows, part),
    )
    levels = lax.all_to_all(levels.reshape(pops, rows, part), POP, 0, 0, tiled=True)
    levels = levels.reshape(pops * rows, part)
    first, second = call(
        functools.partial(pack_kernel, blocks, steps),
        (struct((40, cols), I16), struct((40, cols), I16)),
        levels,
        terminal,
    )
    second = second_swap(second)
    first = first_swap(first)
    fields, edges, sums = call(
        functools.partial(backward_kernel, blocks, steps),
        (
            struct((steps, 3 * HALO, cols), F32),
            struct((32, cols), F32),
            struct((tiles, 1, 128), F32),
        ),
        weights,
        levels,
        terminal,
        init,
        first,
        second,
    )
    first = first_swap(edges)
    second = second_swap(edges)
    sums = lax.all_to_all(sums, "tile", 0, 0, tiled=True)
    final = call(
        functools.partial(forward_kernel, steps),
        struct((rows, cols), F32),
        fields,
        init,
        second,
        first,
    )
    sums, final = lax.optimization_barrier((sums, final))
    values = call(
        functools.partial(centre_kernel, float(tiles * rows * cols), steps),
        struct((steps, rows, cols), F32),
        fields,
        sums,
    )
    return values[None], final[None]


def solution(mesh):
    split = Mesh(
        mesh.devices.reshape(8, 2, 2, mesh.shape["tile"]), ("pop_0", "pop_1", "pop_2", "tile")
    )
    in_specs = (P(), P(POP, "tile", None), P(POP, None, "tile", None), P(POP, "tile", None))
    out_specs = (P(POP, None, "tile", None), P(POP, "tile", None))
    return jax.shard_map(
        per_device, mesh=split, in_specs=in_specs, out_specs=out_specs, check_vma=False
    )
```

```python
import functools

import jax
import jax.numpy as jnp
from jax import lax
from jax.experimental import pallas as pl
from jax.experimental.pallas import tpu as pltpu
from jax.sharding import Mesh
from jax.sharding import PartitionSpec as P

POP = ("pop_0", "pop_1", "pop_2")

time_step = 0.2
viscosity = 0.2

DENSITY_MID = (0.19921875 + 2.0) / 2
DENSITY_HALF = (2.0 - 0.19921875) / 2
LEVELS = 32000.0
TERMINAL_SCALE = 32000.0 / 4.5
INIT_MID = 1.1
INIT_SCALE = 32000.0 / 0.9

HALO = 8
F32 = jnp.float32
I16 = jnp.int16


def to_i16(x):
    return jnp.round(x).astype(jnp.int32).astype(I16)


def spread_kernel(w_ref, kron_ref, scale_ref):
    pops = w_ref.shape[0]
    rows = kron_ref.shape[0]
    per = rows // pops
    shift = per.bit_length() - 1
    weights = w_ref[...].astype(F32).astype(jnp.bfloat16)
    i = lax.broadcasted_iota(jnp.int32, (rows, pops), 0)
    q = lax.broadcasted_iota(jnp.int32, (rows, pops), 1)
    spread = jnp.where((i >> shift) == q, 1.0, 0.0).astype(jnp.bfloat16)
    tall = jnp.dot(spread, weights, preferred_element_type=F32)
    total = jnp.sum(tall, axis=1, keepdims=True)
    size = jnp.maximum(jnp.sum(jnp.abs(tall), axis=1, keepdims=True), 1.0)
    wide = lax.dot_general(
        tall.astype(jnp.bfloat16), spread, (((1,), (1,)), ((), ())), preferred_element_type=F32
    )
    a = lax.broadcasted_iota(jnp.int32, (rows, rows), 0)
    b = lax.broadcasted_iota(jnp.int32, (rows, rows), 1)
    kron_ref[...] = jnp.where((a & (per - 1)) == (b & (per - 1)), wide, 0.0).astype(jnp.bfloat16)
    lane = lax.broadcasted_iota(jnp.int32, scale_ref.shape, 1)
    scale_ref[...] = jnp.where(
        lane == 0, DENSITY_MID * total, LEVELS / (DENSITY_HALF * size)
    )


def coupling_kernel(kron_ref, scale_ref, x_ref, out_ref):
    product = jnp.dot(kron_ref[...], x_ref[...], preferred_element_type=F32)
    out_ref[...] = to_i16((product - scale_ref[:, 0:1]) * scale_ref[:, 1:2])


def rows_of_step(wide, step, blocks):
    first = step * blocks * HALO
    return jnp.concatenate(
        [wide[first + k * HALO : first + (k + 1) * HALO] for k in range(blocks)], axis=1
    )


def is_even():
    return (lax.axis_index("tile") & 1) == 0


def pack_kernel(blocks, steps, c_ref, terminal_ref, first_ref, second_ref):
    wide = c_ref[...].astype(F32)
    c = [rows_of_step(wide, t, blocks) for t in range(steps)]
    row = lax.broadcasted_iota(jnp.int32, c[0].shape, 0)
    down = []
    up = []
    for t in range(1, HALO // 2):
        down.append(jnp.where(row >= t, c[HALO - t], pltpu.roll(c[t], t, 0)))
        up.append(jnp.where(row < HALO - t, c[HALO - t], pltpu.roll(c[t], HALO - t, 0)))
    even = is_even()
    edge = terminal_ref[...] * TERMINAL_SCALE
    first = [jnp.where(even, d, u) for d, u in zip(down, up)] + [c[HALO // 2], edge]
    second = [jnp.where(even, u, d) for d, u in zip(down, up)] + [c[HALO // 2], edge]
    first_ref[...] = to_i16(jnp.concatenate(first, axis=0))
    second_ref[...] = to_i16(jnp.concatenate(second, axis=0))


def backward_kernel(
    blocks, steps, w_ref, c_ref, terminal_ref, init_ref, first_ref, second_ref, u_ref, edge_ref, sums_ref
):
    pops = w_ref.shape[0]
    cols = terminal_ref.shape[1]
    own = lax.axis_index(POP)
    own_weights = w_ref[pl.ds(own, 1), :].astype(F32)
    total = jnp.sum(own_weights, axis=1, keepdims=True)
    size = jnp.maximum(jnp.sum(jnp.abs(own_weights), axis=1, keepdims=True), 1.0)
    slope = size * (DENSITY_HALF / (LEVELS * pops))
    offset = total * (DENSITY_MID / pops)
    wide = c_ref[...].astype(F32)
    even = is_even()
    first = first_ref[...].astype(F32)
    second = second_ref[...].astype(F32)
    above = jnp.where(even, second, first)
    below = jnp.where(even, first, second)

    def tile(x, k):
        return x[k * HALO : (k + 1) * HALO]

    def levels(t):
        if t == 0:
            top = bottom = jnp.zeros((HALO, cols), F32)
        elif t <= HALO // 2:
            top = tile(above, t - 1)
            bottom = tile(below, t - 1)
            if t < HALO // 2:
                top = pltpu.roll(top, HALO - t, 0)
                bottom = pltpu.roll(bottom, t, 0)
        else:
            top = tile(above, HALO - t - 1)
            bottom = tile(below, HALO - t - 1)
        return jnp.concatenate([top, rows_of_step(wide, t, blocks), bottom], axis=0)

    last = HALO // 2
    u = jnp.concatenate(
        [
            tile(above, last) * (1.0 / TERMINAL_SCALE),
            terminal_ref[...],
            tile(below, last) * (1.0 / TERMINAL_SCALE),
        ],
        axis=0,
    )
    high = u.shape[0]
    partial = [None] * steps
    kept = [None] * steps
    for t in reversed(range(steps)):
        coupled = levels(t) * slope + offset
        behind_r = u - pltpu.roll(u, 1, 0)
        ahead_r = pltpu.roll(u, high - 1, 0) - u
        behind_c = u - pltpu.roll(u, 1, 1)
        ahead_c = pltpu.roll(u, cols - 1, 1) - u
        lap = (ahead_r - behind_r) + (ahead_c - behind_c)
        br = jnp.maximum(behind_r, 0.0)
        ar = jnp.minimum(ahead_r, 0.0)
        bc = jnp.maximum(behind_c, 0.0)
        ac = jnp.minimum(ahead_c, 0.0)
        ham = 0.5 * (br * br + ar * ar + bc * bc + ac * ac)
        u = u + time_step * (viscosity * lap - ham + coupled)
        u_ref[t] = u
        mine = u[HALO : 2 * HALO]
        kept[t] = mine
        lanes = mine[:, :128]
        for k in range(1, cols // 128):
            lanes = lanes + mine[:, k * 128 : (k + 1) * 128]
        partial[t] = jnp.sum(lanes, axis=0, keepdims=True)
    sums = jnp.sum(jnp.concatenate(partial, axis=0), axis=1, keepdims=True)
    lane = lax.broadcasted_iota(jnp.int32, (steps, 128), 1)
    step = lax.broadcasted_iota(jnp.int32, (steps, 128), 0)
    line = jnp.sum(jnp.where(lane == step, sums, 0.0), axis=0, keepdims=True)
    sums_ref[...] = jnp.broadcast_to(line[None], sums_ref.shape)
    row = lax.broadcasted_iota(jnp.int32, (HALO, cols), 0)
    largest = jnp.maximum(
        jnp.maximum(jnp.abs(kept[0]), jnp.abs(kept[1])),
        jnp.maximum(jnp.abs(kept[2]), jnp.abs(kept[3])),
    )
    largest = jnp.max(jnp.max(largest, axis=1, keepdims=True), axis=0, keepdims=True)
    exponent = jnp.ceil(jnp.log2(jnp.maximum(largest, 1e-30)))
    scale = LEVELS / jnp.exp2(exponent)
    inner = jnp.where((row >= 1) & (row <= 6), kept[1], pltpu.roll(kept[3], 4, 0))
    edge_ref[...] = to_i16(
        jnp.concatenate(
            [
                (init_ref[...] - INIT_MID) * INIT_SCALE,
                kept[0] * scale,
                inner * scale,
                jnp.where(row == 0, exponent, kept[2] * scale),
            ],
            axis=0,
        )
    )


def decoded(edge):
    edge = edge.astype(F32)
    size = jnp.exp2(edge[24:25, 0:1]) * (1.0 / LEVELS)
    return jnp.concatenate([edge[0:8] * (1.0 / INIT_SCALE) + INIT_MID, edge[8:32] * size], axis=0)


def forward_kernel(
    steps, u_ref, init_ref, second_ref, first_ref, final_ref
):
    cols = init_ref.shape[1]
    row = lax.broadcasted_iota(jnp.int32, (HALO, cols), 0)
    even = is_even()
    first = decoded(first_ref[...])
    second = decoded(second_ref[...])
    above = jnp.where(even, second, first)
    below = jnp.where(even, first, second)
    m = jnp.concatenate([above[0:8], init_ref[...], below[0:8]], axis=0)
    high = m.shape[0]

    def field(t):
        u = u_ref[t]
        if t > 3:
            return u

        def side(far, near):
            if t == 0:
                return far[8:16]
            if t == 1:
                return jnp.where((row >= 1) & (row <= 6), far[16:24], near)
            if t == 2:
                return jnp.where((row >= 2) & (row <= 5), far[24:32], near)
            return jnp.where((row >= 3) & (row <= 4), pltpu.roll(far[16:24], 4, 0), near)

        return jnp.concatenate(
            [side(above, u[0:8]), u[8:16], side(below, u[16:24])], axis=0
        )

    for t in range(steps):
        u = field(t)
        down_m = pltpu.roll(m, high - 1, 0)
        right_m = pltpu.roll(m, cols - 1, 1)
        drift_r = u - pltpu.roll(u, high - 1, 0)
        drift_c = u - pltpu.roll(u, cols - 1, 1)
        flux_r = (
            jnp.maximum(drift_r, 0.0) * m
            + jnp.minimum(drift_r, 0.0) * down_m
            - viscosity * (down_m - m)
        )
        flux_c = (
            jnp.maximum(drift_c, 0.0) * m
            + jnp.minimum(drift_c, 0.0) * right_m
            - viscosity * (right_m - m)
        )
        m = m - time_step * (
            (flux_r - pltpu.roll(flux_r, 1, 0)) + (flux_c - pltpu.roll(flux_c, 1, 1))
        )
    final_ref[...] = m[HALO : 2 * HALO]


def centre_kernel(cells, steps, u_ref, sums_ref, values_ref):
    means = jnp.sum(sums_ref[:, 0:1, :], axis=0) * (1.0 / cells)
    for t in range(steps):
        values_ref[t] = u_ref[t, HALO : 2 * HALO, :] - means[:, t : t + 1]


def call(kernel, outs, *args):
    spec = pl.BlockSpec(memory_space=pltpu.VMEM)
    return pl.pallas_call(
        kernel,
        out_shape=outs,
        in_specs=[spec] * len(args),
        out_specs=jax.tree.map(lambda _: spec, outs),
        compiler_params=pltpu.CompilerParams(vmem_limit_bytes=40 * 1024 * 1024),
    )(*args)


def first_swap(x):
    peers = lax.axis_size("tile")
    return lax.ppermute(x, "tile", [(i, i ^ 1) for i in range(peers)])


def second_swap(x):
    peers = lax.axis_size("tile")
    return lax.ppermute(x, "tile", [(i, (((i + 1) ^ 1) - 1) % peers) for i in range(peers)])


def per_device(weights, terminal, density_history, density_init):
    pops = weights.shape[0]
    steps, rows, cols = density_history.shape[1:]
    tiles = lax.axis_size("tile")
    blocks = pops // steps
    part = cols // blocks
    struct = jax.ShapeDtypeStruct
    terminal = terminal[0]
    init = density_init[0]
    chunks = density_history[0].reshape(steps, rows, blocks, part).transpose(0, 2, 1, 3)
    chunks = lax.all_to_all(chunks.reshape(pops, rows, part), POP, 0, 0, tiled=True)
    kron, scale = call(
        spread_kernel,
        (struct((pops * rows, pops * rows), jnp.bfloat16), struct((pops * rows, 128), F32)),
        weights,
    )
    levels = call(
        coupling_kernel,
        struct((pops * rows, part), I16),
        kron,
        scale,
        chunks.reshape(pops * rows, part),
    )
    levels = lax.all_to_all(levels.reshape(pops, rows, part), POP, 0, 0, tiled=True)
    levels = levels.reshape(pops * rows, part)
    first, second = call(
        functools.partial(pack_kernel, blocks, steps),
        (struct((40, cols), I16), struct((40, cols), I16)),
        levels,
        terminal,
    )
    second = second_swap(second)
    first = first_swap(first)
    fields, edges, sums = call(
        functools.partial(backward_kernel, blocks, steps),
        (
            struct((steps, 3 * HALO, cols), F32),
            struct((32, cols), I16),
            struct((tiles, 16, 128), F32),
        ),
        weights,
        levels,
        terminal,
        init,
        first,
        second,
    )
    first = first_swap(edges)
    second = second_swap(edges)
    sums = lax.all_to_all(sums, "tile", 0, 0, tiled=True)
    final = call(
        functools.partial(forward_kernel, steps),
        struct((rows, cols), F32),
        fields,
        init,
        second,
        first,
    )
    sums, final = lax.optimization_barrier((sums, final))
    values = call(
        functools.partial(centre_kernel, float(tiles * rows * cols), steps),
        struct((steps, rows, cols), F32),
        fields,
        sums,
    )
    return values[None], final[None]


def solution(mesh):
    split = Mesh(
        mesh.devices.reshape(8, 2, 2, mesh.shape["tile"]), ("pop_0", "pop_1", "pop_2", "tile")
    )
    in_specs = (P(), P(POP, "tile", None), P(POP, None, "tile", None), P(POP, "tile", None))
    out_specs = (P(POP, None, "tile", None), P(POP, "tile", None))
    return jax.shard_map(
        per_device, mesh=split, in_specs=in_specs, out_specs=out_specs, check_vma=False
    )
```

```python
import functools

import jax
import jax.numpy as jnp
from jax import lax
from jax.experimental import pallas as pl
from jax.experimental.pallas import tpu as pltpu
from jax.sharding import Mesh
from jax.sharding import PartitionSpec as P

POP = ("pop_0", "pop_1", "pop_2")

time_step = 0.2
viscosity = 0.2

DENSITY_MID = (0.19921875 + 2.0) / 2
DENSITY_HALF = (2.0 - 0.19921875) / 2
LEVELS = 32000.0
TERMINAL_SCALE = 32000.0 / 4.5
INIT_MID = 1.1
INIT_SCALE = 32000.0 / 0.9

HALO = 8
F32 = jnp.float32
I16 = jnp.int16


def to_i16(x):
    return jnp.round(x).astype(jnp.int32).astype(I16)


def spread_kernel(w_ref, kron_ref, scale_ref):
    pops = w_ref.shape[0]
    rows = kron_ref.shape[0]
    per = rows // pops
    shift = per.bit_length() - 1
    weights = w_ref[...].astype(F32).astype(jnp.bfloat16)
    i = lax.broadcasted_iota(jnp.int32, (rows, pops), 0)
    q = lax.broadcasted_iota(jnp.int32, (rows, pops), 1)
    spread = jnp.where((i >> shift) == q, 1.0, 0.0).astype(jnp.bfloat16)
    tall = jnp.dot(spread, weights, preferred_element_type=F32)
    total = jnp.sum(tall, axis=1, keepdims=True)
    size = jnp.maximum(jnp.sum(jnp.abs(tall), axis=1, keepdims=True), 1.0)
    wide = lax.dot_general(
        tall.astype(jnp.bfloat16), spread, (((1,), (1,)), ((), ())), preferred_element_type=F32
    )
    a = lax.broadcasted_iota(jnp.int32, (rows, rows), 0)
    b = lax.broadcasted_iota(jnp.int32, (rows, rows), 1)
    kron_ref[...] = jnp.where((a & (per - 1)) == (b & (per - 1)), wide, 0.0).astype(jnp.bfloat16)
    lane = lax.broadcasted_iota(jnp.int32, scale_ref.shape, 1)
    scale_ref[...] = jnp.where(
        lane == 0, DENSITY_MID * total, LEVELS / (DENSITY_HALF * size)
    )


def coupling_kernel(kron_ref, scale_ref, x_ref, out_ref):
    product = jnp.dot(kron_ref[...], x_ref[...], preferred_element_type=F32)
    out_ref[...] = to_i16((product - scale_ref[:, 0:1]) * scale_ref[:, 1:2])


def rows_of_step(wide, step, blocks):
    first = step * blocks * HALO
    return jnp.concatenate(
        [wide[first + k * HALO : first + (k + 1) * HALO] for k in range(blocks)], axis=1
    )


def is_even():
    return (lax.axis_index("tile") & 1) == 0


def pack_kernel(blocks, steps, c_ref, terminal_ref, first_ref, second_ref):
    wide = c_ref[...].astype(F32)
    c = [rows_of_step(wide, t, blocks) for t in range(steps)]
    row = lax.broadcasted_iota(jnp.int32, c[0].shape, 0)
    down = []
    up = []
    for t in range(1, HALO // 2):
        down.append(jnp.where(row >= t, c[HALO - t], pltpu.roll(c[t], t, 0)))
        up.append(jnp.where(row < HALO - t, c[HALO - t], pltpu.roll(c[t], HALO - t, 0)))
    even = is_even()
    edge = terminal_ref[...] * TERMINAL_SCALE
    first = [jnp.where(even, d, u) for d, u in zip(down, up)] + [c[HALO // 2], edge]
    second = [jnp.where(even, u, d) for d, u in zip(down, up)] + [c[HALO // 2], edge]
    first_ref[...] = to_i16(jnp.concatenate(first, axis=0))
    second_ref[...] = to_i16(jnp.concatenate(second, axis=0))


def backward_kernel(
    blocks, steps, w_ref, c_ref, terminal_ref, init_ref, first_ref, second_ref, u_ref, first_edge_ref, second_edge_ref, sums_ref
):
    pops = w_ref.shape[0]
    cols = terminal_ref.shape[1]
    own = lax.axis_index(POP)
    own_weights = w_ref[pl.ds(own, 1), :].astype(F32)
    total = jnp.sum(own_weights, axis=1, keepdims=True)
    size = jnp.maximum(jnp.sum(jnp.abs(own_weights), axis=1, keepdims=True), 1.0)
    slope = size * (DENSITY_HALF / (LEVELS * pops))
    offset = total * (DENSITY_MID / pops)
    wide = c_ref[...].astype(F32)
    even = is_even()
    first = first_ref[...].astype(F32)
    second = second_ref[...].astype(F32)
    above = jnp.where(even, second, first)
    below = jnp.where(even, first, second)

    def tile(x, k):
        return x[k * HALO : (k + 1) * HALO]

    def levels(t):
        if t == 0:
            top = bottom = jnp.zeros((HALO, cols), F32)
        elif t <= HALO // 2:
            top = tile(above, t - 1)
            bottom = tile(below, t - 1)
            if t < HALO // 2:
                top = pltpu.roll(top, HALO - t, 0)
                bottom = pltpu.roll(bottom, t, 0)
        else:
            top = tile(above, HALO - t - 1)
            bottom = tile(below, HALO - t - 1)
        return jnp.concatenate([top, rows_of_step(wide, t, blocks), bottom], axis=0)

    last = HALO // 2
    u = jnp.concatenate(
        [
            tile(above, last) * (1.0 / TERMINAL_SCALE),
            terminal_ref[...],
            tile(below, last) * (1.0 / TERMINAL_SCALE),
        ],
        axis=0,
    )
    high = u.shape[0]
    partial = [None] * steps
    kept = [None] * steps
    for t in reversed(range(steps)):
        coupled = levels(t) * slope + offset
        behind_r = u - pltpu.roll(u, 1, 0)
        ahead_r = pltpu.roll(u, high - 1, 0) - u
        behind_c = u - pltpu.roll(u, 1, 1)
        ahead_c = pltpu.roll(u, cols - 1, 1) - u
        lap = (ahead_r - behind_r) + (ahead_c - behind_c)
        br = jnp.maximum(behind_r, 0.0)
        ar = jnp.minimum(ahead_r, 0.0)
        bc = jnp.maximum(behind_c, 0.0)
        ac = jnp.minimum(ahead_c, 0.0)
        ham = 0.5 * (br * br + ar * ar + bc * bc + ac * ac)
        u = u + time_step * (viscosity * lap - ham + coupled)
        u_ref[t] = u
        mine = u[HALO : 2 * HALO]
        kept[t] = mine
        lanes = mine[:, :128]
        for k in range(1, cols // 128):
            lanes = lanes + mine[:, k * 128 : (k + 1) * 128]
        partial[t] = jnp.sum(lanes, axis=0, keepdims=True)
    sums = jnp.sum(jnp.concatenate(partial, axis=0), axis=1, keepdims=True)
    lane = lax.broadcasted_iota(jnp.int32, (steps, 128), 1)
    step = lax.broadcasted_iota(jnp.int32, (steps, 128), 0)
    line = jnp.sum(jnp.where(lane == step, sums, 0.0), axis=0, keepdims=True)
    sums_ref[...] = jnp.broadcast_to(
        jnp.concatenate([line] * (sums_ref.shape[2] // 128), axis=1)[None], sums_ref.shape
    )
    row = lax.broadcasted_iota(jnp.int32, (HALO, cols), 0)
    largest = jnp.maximum(
        jnp.maximum(jnp.abs(kept[0]), jnp.abs(kept[1])),
        jnp.maximum(jnp.abs(kept[2]), jnp.abs(kept[3])),
    )
    largest = jnp.max(jnp.max(largest, axis=1, keepdims=True), axis=0, keepdims=True)
    exponent = jnp.ceil(jnp.log2(jnp.maximum(largest, 1e-30)))
    scale = LEVELS / jnp.exp2(exponent)
    inner = jnp.where((row >= 1) & (row <= 6), kept[1], pltpu.roll(kept[3], 4, 0))
    first_edge_ref[0:8] = init_ref[...]
    first_edge_ref[8:16] = kept[0]
    first_edge_ref[16:24] = inner
    first_edge_ref[24:32] = kept[2]
    second_edge_ref[...] = to_i16(
        jnp.concatenate(
            [
                (init_ref[...] - INIT_MID) * INIT_SCALE,
                kept[0] * scale,
                inner * scale,
                jnp.where(row == 0, exponent, kept[2] * scale),
            ],
            axis=0,
        )
    )


def decoded(edge):
    edge = edge.astype(F32)
    size = jnp.exp2(edge[24:25, 0:1]) * (1.0 / LEVELS)
    return jnp.concatenate([edge[0:8] * (1.0 / INIT_SCALE) + INIT_MID, edge[8:32] * size], axis=0)


def forward_kernel(
    steps, u_ref, init_ref, second_ref, first_ref, final_ref
):
    cols = init_ref.shape[1]
    row = lax.broadcasted_iota(jnp.int32, (HALO, cols), 0)
    even = is_even()
    first = first_ref[...]
    second = decoded(second_ref[...])
    above = jnp.where(even, second, first)
    below = jnp.where(even, first, second)
    m = jnp.concatenate([above[0:8], init_ref[...], below[0:8]], axis=0)
    high = m.shape[0]

    def field(t):
        u = u_ref[t]
        if t > 3:
            return u

        def side(far, near):
            if t == 0:
                return far[8:16]
            if t == 1:
                return jnp.where((row >= 1) & (row <= 6), far[16:24], near)
            if t == 2:
                return jnp.where((row >= 2) & (row <= 5), far[24:32], near)
            return jnp.where((row >= 3) & (row <= 4), pltpu.roll(far[16:24], 4, 0), near)

        return jnp.concatenate(
            [side(above, u[0:8]), u[8:16], side(below, u[16:24])], axis=0
        )

    for t in range(steps):
        u = field(t)
        down_m = pltpu.roll(m, high - 1, 0)
        right_m = pltpu.roll(m, cols - 1, 1)
        drift_r = u - pltpu.roll(u, high - 1, 0)
        drift_c = u - pltpu.roll(u, cols - 1, 1)
        flux_r = (
            jnp.maximum(drift_r, 0.0) * m
            + jnp.minimum(drift_r, 0.0) * down_m
            - viscosity * (down_m - m)
        )
        flux_c = (
            jnp.maximum(drift_c, 0.0) * m
            + jnp.minimum(drift_c, 0.0) * right_m
            - viscosity * (right_m - m)
        )
        m = m - time_step * (
            (flux_r - pltpu.roll(flux_r, 1, 0)) + (flux_c - pltpu.roll(flux_c, 1, 1))
        )
    final_ref[...] = m[HALO : 2 * HALO]


def centre_kernel(cells, steps, u_ref, sums_ref, values_ref):
    means = jnp.sum(sums_ref[:, :, 0:128], axis=0) * (1.0 / cells)
    for t in range(steps):
        values_ref[t] = u_ref[t, HALO : 2 * HALO, :] - means[:, t : t + 1]


def call(kernel, outs, *args):
    spec = pl.BlockSpec(memory_space=pltpu.VMEM)
    return pl.pallas_call(
        kernel,
        out_shape=outs,
        in_specs=[spec] * len(args),
        out_specs=jax.tree.map(lambda _: spec, outs),
        compiler_params=pltpu.CompilerParams(vmem_limit_bytes=40 * 1024 * 1024),
    )(*args)


def first_swap(x):
    peers = lax.axis_size("tile")
    return lax.ppermute(x, "tile", [(i, i ^ 1) for i in range(peers)])


def second_swap(x):
    peers = lax.axis_size("tile")
    return lax.ppermute(x, "tile", [(i, (((i + 1) ^ 1) - 1) % peers) for i in range(peers)])


def per_device(weights, terminal, density_history, density_init):
    pops = weights.shape[0]
    steps, rows, cols = density_history.shape[1:]
    tiles = lax.axis_size("tile")
    blocks = pops // steps
    part = cols // blocks
    struct = jax.ShapeDtypeStruct
    terminal = terminal[0]
    init = density_init[0]
    chunks = density_history[0].reshape(steps, rows, blocks, part).transpose(0, 2, 1, 3)
    chunks = lax.all_to_all(chunks.reshape(pops, rows, part), POP, 0, 0, tiled=True)
    kron, scale = call(
        spread_kernel,
        (struct((pops * rows, pops * rows), jnp.bfloat16), struct((pops * rows, 128), F32)),
        weights,
    )
    levels = call(
        coupling_kernel,
        struct((pops * rows, part), I16),
        kron,
        scale,
        chunks.reshape(pops * rows, part),
    )
    levels = lax.all_to_all(levels.reshape(pops, rows, part), POP, 0, 0, tiled=True)
    levels = levels.reshape(pops * rows, part)
    first, second = call(
        functools.partial(pack_kernel, blocks, steps),
        (struct((40, cols), I16), struct((40, cols), I16)),
        levels,
        terminal,
    )
    second = second_swap(second)
    first = first_swap(first)
    fields, first, second, sums = call(
        functools.partial(backward_kernel, blocks, steps),
        (
            struct((steps, 3 * HALO, cols), F32),
            struct((32, cols), F32),
            struct((32, cols), I16),
            struct((tiles, 1, 1152), F32),
        ),
        weights,
        levels,
        terminal,
        init,
        first,
        second,
    )
    first = first_swap(first)
    second = second_swap(second)
    sums = lax.all_to_all(sums, "tile", 0, 0, tiled=True)
    final = call(
        functools.partial(forward_kernel, steps),
        struct((rows, cols), F32),
        fields,
        init,
        second,
        first,
    )
    sums, final = lax.optimization_barrier((sums, final))
    values = call(
        functools.partial(centre_kernel, float(tiles * rows * cols), steps),
        struct((steps, rows, cols), F32),
        fields,
        sums,
    )
    return values[None], final[None]


def solution(mesh):
    split = Mesh(
        mesh.devices.reshape(8, 2, 2, mesh.shape["tile"]), ("pop_0", "pop_1", "pop_2", "tile")
    )
    in_specs = (P(), P(POP, "tile", None), P(POP, None, "tile", None), P(POP, "tile", None))
    out_specs = (P(POP, None, "tile", None), P(POP, "tile", None))
    return jax.shard_map(
        per_device, mesh=split, in_specs=in_specs, out_specs=out_specs, check_vma=False
    )
```

```python
import functools

import jax
import jax.numpy as jnp
from jax import lax
from jax.experimental import pallas as pl
from jax.experimental.pallas import tpu as pltpu
from jax.sharding import Mesh
from jax.sharding import PartitionSpec as P

POP = ("pop_0", "pop_1", "pop_2")

time_step = 0.2
viscosity = 0.2

DENSITY_MID = (0.19921875 + 2.0) / 2
DENSITY_HALF = (2.0 - 0.19921875) / 2
LEVELS = 32000.0
TERMINAL_SCALE = 32000.0 / 4.5
INIT_MID = 1.1
INIT_SCALE = 32000.0 / 0.9

HALO = 8
KAPPA = time_step / 2

F32 = jnp.float32
I16 = jnp.int16


def to_i16(x):
    return jnp.round(x).astype(jnp.int32).astype(I16)


def spread_kernel(w_ref, kron_ref, scale_ref):
    pops = w_ref.shape[0]
    rows = kron_ref.shape[0]
    per = rows // pops
    shift = per.bit_length() - 1
    weights = w_ref[...].astype(F32).astype(jnp.bfloat16)
    i = lax.broadcasted_iota(jnp.int32, (rows, pops), 0)
    q = lax.broadcasted_iota(jnp.int32, (rows, pops), 1)
    spread = jnp.where((i >> shift) == q, 1.0, 0.0).astype(jnp.bfloat16)
    tall = jnp.dot(spread, weights, preferred_element_type=F32)
    total = jnp.sum(tall, axis=1, keepdims=True)
    size = jnp.maximum(jnp.sum(jnp.abs(tall), axis=1, keepdims=True), 1.0)
    wide = lax.dot_general(
        tall.astype(jnp.bfloat16), spread, (((1,), (1,)), ((), ())), preferred_element_type=F32
    )
    a = lax.broadcasted_iota(jnp.int32, (rows, rows), 0)
    b = lax.broadcasted_iota(jnp.int32, (rows, rows), 1)
    kron_ref[...] = jnp.where((a & (per - 1)) == (b & (per - 1)), wide, 0.0).astype(jnp.bfloat16)
    lane = lax.broadcasted_iota(jnp.int32, scale_ref.shape, 1)
    scale_ref[...] = jnp.where(
        lane == 0, DENSITY_MID * total, LEVELS / (DENSITY_HALF * size)
    )


def coupling_kernel(kron_ref, scale_ref, x_ref, out_ref):
    product = jnp.dot(kron_ref[...], x_ref[...], preferred_element_type=F32)
    out_ref[...] = to_i16((product - scale_ref[:, 0:1]) * scale_ref[:, 1:2])


def rows_of_step(wide, step, blocks):
    first = step * blocks * HALO
    return jnp.concatenate(
        [wide[first + k * HALO : first + (k + 1) * HALO] for k in range(blocks)], axis=1
    )


def is_even():
    return (lax.axis_index("tile") & 1) == 0


def pack_kernel(blocks, steps, c_ref, terminal_ref, first_ref, second_ref):
    wide = c_ref[...].astype(F32)
    c = [rows_of_step(wide, t, blocks) for t in range(steps)]
    row = lax.broadcasted_iota(jnp.int32, c[0].shape, 0)
    down = []
    up = []
    for t in range(1, HALO // 2):
        down.append(jnp.where(row >= t, c[HALO - t], pltpu.roll(c[t], t, 0)))
        up.append(jnp.where(row < HALO - t, c[HALO - t], pltpu.roll(c[t], HALO - t, 0)))
    even = is_even()
    edge = terminal_ref[...] * TERMINAL_SCALE
    first = [jnp.where(even, d, u) for d, u in zip(down, up)] + [c[HALO // 2], edge]
    second = [jnp.where(even, u, d) for d, u in zip(down, up)] + [c[HALO // 2], edge]
    first_ref[...] = to_i16(jnp.concatenate(first, axis=0))
    second_ref[...] = to_i16(jnp.concatenate(second, axis=0))


def shares(ahead):
    falling = jnp.minimum(ahead, 0.0)
    low = (time_step * viscosity) * ahead - falling * falling
    return low, ahead * ahead + low


def flux(drift, m, beyond):
    return (jnp.maximum(drift, 0.0) + KAPPA * viscosity) * (m - beyond) + drift * beyond


def backward_kernel(
    blocks, steps, w_ref, c_ref, terminal_ref, init_ref, first_ref, second_ref, u_ref, first_edge_ref, second_edge_ref, sums_ref
):
    pops = w_ref.shape[0]
    cols = terminal_ref.shape[1]
    own = lax.axis_index(POP)
    own_weights = w_ref[pl.ds(own, 1), :].astype(F32)
    total = jnp.sum(own_weights, axis=1, keepdims=True)
    size = jnp.maximum(jnp.sum(jnp.abs(own_weights), axis=1, keepdims=True), 1.0)
    slope = size * (KAPPA * time_step * DENSITY_HALF / (LEVELS * pops))
    offset = total * (KAPPA * time_step * DENSITY_MID / pops)
    wide = c_ref[...].astype(F32)
    even = is_even()
    first = first_ref[...].astype(F32)
    second = second_ref[...].astype(F32)
    above = jnp.where(even, second, first)
    below = jnp.where(even, first, second)

    def tile(x, k):
        return x[k * HALO : (k + 1) * HALO]

    def levels(t):
        if t == 0:
            top = bottom = jnp.zeros((HALO, cols), F32)
        elif t <= HALO // 2:
            top = tile(above, t - 1)
            bottom = tile(below, t - 1)
            if t < HALO // 2:
                top = pltpu.roll(top, HALO - t, 0)
                bottom = pltpu.roll(bottom, t, 0)
        else:
            top = tile(above, HALO - t - 1)
            bottom = tile(below, HALO - t - 1)
        return jnp.concatenate([top, rows_of_step(wide, t, blocks), bottom], axis=0)

    last = HALO // 2
    u = jnp.concatenate(
        [
            tile(above, last) * (KAPPA / TERMINAL_SCALE),
            terminal_ref[...] * KAPPA,
            tile(below, last) * (KAPPA / TERMINAL_SCALE),
        ],
        axis=0,
    )
    high = u.shape[0]
    partial = [None] * steps
    kept = [None] * steps
    for t in reversed(range(steps)):
        ahead_r = pltpu.roll(u, high - 1, 0) - u
        ahead_c = pltpu.roll(u, cols - 1, 1) - u
        low_r, up_r = shares(ahead_r)
        low_c, up_c = shares(ahead_c)
        source = levels(t) * slope + offset
        u = (u + source) + (low_r - pltpu.roll(up_r, 1, 0)) + (low_c - pltpu.roll(up_c, 1, 1))
        u_ref[t] = u
        mine = u[HALO : 2 * HALO]
        kept[t] = mine
        lanes = mine[:, :128]
        for k in range(1, cols // 128):
            lanes = lanes + mine[:, k * 128 : (k + 1) * 128]
        partial[t] = jnp.sum(lanes, axis=0, keepdims=True)
    sums = jnp.sum(jnp.concatenate(partial, axis=0), axis=1, keepdims=True)
    lane = lax.broadcasted_iota(jnp.int32, (steps, 128), 1)
    step = lax.broadcasted_iota(jnp.int32, (steps, 128), 0)
    line = jnp.sum(jnp.where(lane == step, sums, 0.0), axis=0, keepdims=True)
    sums_ref[...] = jnp.broadcast_to(
        jnp.concatenate([line] * (sums_ref.shape[2] // 128), axis=1)[None], sums_ref.shape
    )
    row = lax.broadcasted_iota(jnp.int32, (HALO, cols), 0)
    largest = jnp.maximum(
        jnp.maximum(jnp.abs(kept[0]), jnp.abs(kept[1])),
        jnp.maximum(jnp.abs(kept[2]), jnp.abs(kept[3])),
    )
    largest = jnp.max(jnp.max(largest, axis=1, keepdims=True), axis=0, keepdims=True)
    exponent = jnp.ceil(jnp.log2(jnp.maximum(largest, 1e-30)))
    scale = LEVELS / jnp.exp2(exponent)
    inner = jnp.where((row >= 1) & (row <= 6), kept[1], pltpu.roll(kept[3], 4, 0))
    first_edge_ref[0:8] = init_ref[...]
    first_edge_ref[8:16] = kept[0]
    first_edge_ref[16:24] = inner
    first_edge_ref[24:32] = kept[2]
    second_edge_ref[...] = to_i16(
        jnp.concatenate(
            [
                (init_ref[...] - INIT_MID) * INIT_SCALE,
                kept[0] * scale,
                inner * scale,
                jnp.where(row == 0, exponent, kept[2] * scale),
            ],
            axis=0,
        )
    )


def decoded(edge):
    edge = edge.astype(F32)
    size = jnp.exp2(edge[24:25, 0:1]) * (1.0 / LEVELS)
    return jnp.concatenate([edge[0:8] * (1.0 / INIT_SCALE) + INIT_MID, edge[8:32] * size], axis=0)


def forward_kernel(
    steps, u_ref, init_ref, second_ref, first_ref, final_ref
):
    cols = init_ref.shape[1]
    row = lax.broadcasted_iota(jnp.int32, (HALO, cols), 0)
    even = is_even()
    first = first_ref[...]
    second = decoded(second_ref[...])
    above = jnp.where(even, second, first)
    below = jnp.where(even, first, second)
    m = jnp.concatenate([above[0:8], init_ref[...], below[0:8]], axis=0)
    high = m.shape[0]

    def field(t):
        u = u_ref[t]
        if t > 3:
            return u

        def side(far, near):
            if t == 0:
                return far[8:16]
            if t == 1:
                return jnp.where((row >= 1) & (row <= 6), far[16:24], near)
            if t == 2:
                return jnp.where((row >= 2) & (row <= 5), far[24:32], near)
            return jnp.where((row >= 3) & (row <= 4), pltpu.roll(far[16:24], 4, 0), near)

        return jnp.concatenate(
            [side(above, u[0:8]), u[8:16], side(below, u[16:24])], axis=0
        )

    for t in range(steps):
        u = field(t)
        down_m = pltpu.roll(m, high - 1, 0)
        right_m = pltpu.roll(m, cols - 1, 1)
        flux_r = flux(u - pltpu.roll(u, high - 1, 0), m, down_m)
        flux_c = flux(u - pltpu.roll(u, cols - 1, 1), m, right_m)
        m = m - (time_step / KAPPA) * (
            (flux_r - pltpu.roll(flux_r, 1, 0)) + (flux_c - pltpu.roll(flux_c, 1, 1))
        )
    final_ref[...] = m[HALO : 2 * HALO]


def centre_kernel(cells, steps, u_ref, sums_ref, values_ref):
    means = jnp.sum(sums_ref[:, :, 0:128], axis=0) * (1.0 / cells)
    for t in range(steps):
        values_ref[t] = (u_ref[t, HALO : 2 * HALO, :] - means[:, t : t + 1]) * (1.0 / KAPPA)


def call(kernel, outs, *args):
    spec = pl.BlockSpec(memory_space=pltpu.VMEM)
    return pl.pallas_call(
        kernel,
        out_shape=outs,
        in_specs=[spec] * len(args),
        out_specs=jax.tree.map(lambda _: spec, outs),
        compiler_params=pltpu.CompilerParams(vmem_limit_bytes=40 * 1024 * 1024),
    )(*args)


def first_swap(x):
    peers = lax.axis_size("tile")
    return lax.ppermute(x, "tile", [(i, i ^ 1) for i in range(peers)])


def second_swap(x):
    peers = lax.axis_size("tile")
    return lax.ppermute(x, "tile", [(i, (((i + 1) ^ 1) - 1) % peers) for i in range(peers)])


def per_device(weights, terminal, density_history, density_init):
    pops = weights.shape[0]
    steps, rows, cols = density_history.shape[1:]
    tiles = lax.axis_size("tile")
    blocks = pops // steps
    part = cols // blocks
    struct = jax.ShapeDtypeStruct
    terminal = terminal[0]
    init = density_init[0]
    chunks = density_history[0].reshape(steps, rows, blocks, part).transpose(0, 2, 1, 3)
    chunks = lax.all_to_all(chunks.reshape(pops, rows, part), POP, 0, 0, tiled=True)
    kron, scale = call(
        spread_kernel,
        (struct((pops * rows, pops * rows), jnp.bfloat16), struct((pops * rows, 128), F32)),
        weights,
    )
    levels = call(
        coupling_kernel,
        struct((pops * rows, part), I16),
        kron,
        scale,
        chunks.reshape(pops * rows, part),
    )
    levels = lax.all_to_all(levels.reshape(pops, rows, part), POP, 0, 0, tiled=True)
    levels = levels.reshape(pops * rows, part)
    first, second = call(
        functools.partial(pack_kernel, blocks, steps),
        (struct((40, cols), I16), struct((40, cols), I16)),
        levels,
        terminal,
    )
    second = second_swap(second)
    first = first_swap(first)
    fields, first, second, sums = call(
        functools.partial(backward_kernel, blocks, steps),
        (
            struct((steps, 3 * HALO, cols), F32),
            struct((32, cols), F32),
            struct((32, cols), I16),
            struct((tiles, 1, 1152), F32),
        ),
        weights,
        levels,
        terminal,
        init,
        first,
        second,
    )
    first = first_swap(first)
    second = second_swap(second)
    sums = lax.all_to_all(sums, "tile", 0, 0, tiled=True)
    final = call(
        functools.partial(forward_kernel, steps),
        struct((rows, cols), F32),
        fields,
        init,
        second,
        first,
    )
    sums, final = lax.optimization_barrier((sums, final))
    values = call(
        functools.partial(centre_kernel, float(tiles * rows * cols), steps),
        struct((steps, rows, cols), F32),
        fields,
        sums,
    )
    return values[None], final[None]


def solution(mesh):
    split = Mesh(
        mesh.devices.reshape(8, 2, 2, mesh.shape["tile"]), ("pop_0", "pop_1", "pop_2", "tile")
    )
    in_specs = (P(), P(POP, "tile", None), P(POP, None, "tile", None), P(POP, "tile", None))
    out_specs = (P(POP, None, "tile", None), P(POP, "tile", None))
    return jax.shard_map(
        per_device, mesh=split, in_specs=in_specs, out_specs=out_specs, check_vma=False
    )
```

```python
import functools

import jax
import jax.numpy as jnp
from jax import lax
from jax.experimental import pallas as pl
from jax.experimental.pallas import tpu as pltpu
from jax.sharding import Mesh
from jax.sharding import PartitionSpec as P

POP = ("pop_0", "pop_1", "pop_2")

time_step = 0.2
viscosity = 0.2

DENSITY_MID = (0.19921875 + 2.0) / 2
DENSITY_HALF = (2.0 - 0.19921875) / 2
LEVELS = 32000.0
TERMINAL_SCALE = 32000.0 / 4.5
INIT_MID = 1.1
INIT_SCALE = 32000.0 / 0.9

HALO = 8
KAPPA = time_step / 2

F32 = jnp.float32
I16 = jnp.int16


def to_i16(x):
    return jnp.round(x).astype(jnp.int32).astype(I16)


def spread_kernel(w_ref, kron_ref, scale_ref):
    pops = w_ref.shape[0]
    rows = kron_ref.shape[0]
    per = rows // pops
    shift = per.bit_length() - 1
    weights = w_ref[...].astype(F32).astype(jnp.bfloat16)
    i = lax.broadcasted_iota(jnp.int32, (rows, pops), 0)
    q = lax.broadcasted_iota(jnp.int32, (rows, pops), 1)
    spread = jnp.where((i >> shift) == q, 1.0, 0.0).astype(jnp.bfloat16)
    tall = jnp.dot(spread, weights, preferred_element_type=F32)
    total = jnp.sum(tall, axis=1, keepdims=True)
    size = jnp.maximum(jnp.sum(jnp.abs(tall), axis=1, keepdims=True), 1.0)
    wide = lax.dot_general(
        tall.astype(jnp.bfloat16), spread, (((1,), (1,)), ((), ())), preferred_element_type=F32
    )
    a = lax.broadcasted_iota(jnp.int32, (rows, rows), 0)
    b = lax.broadcasted_iota(jnp.int32, (rows, rows), 1)
    kron_ref[...] = jnp.where((a & (per - 1)) == (b & (per - 1)), wide, 0.0).astype(jnp.bfloat16)
    lane = lax.broadcasted_iota(jnp.int32, scale_ref.shape, 1)
    scale_ref[...] = jnp.where(
        lane == 0, DENSITY_MID * total, LEVELS / (DENSITY_HALF * size)
    )


def coupling_kernel(kron_ref, scale_ref, x_ref, out_ref):
    product = jnp.dot(kron_ref[...], x_ref[...], preferred_element_type=F32)
    out_ref[...] = to_i16((product - scale_ref[:, 0:1]) * scale_ref[:, 1:2])


def rows_of_step(wide, step, blocks):
    first = step * blocks * HALO
    return jnp.concatenate(
        [wide[first + k * HALO : first + (k + 1) * HALO] for k in range(blocks)], axis=1
    )


def is_even():
    return (lax.axis_index("tile") & 1) == 0


def pack_kernel(blocks, steps, c_ref, terminal_ref, first_ref, second_ref):
    wide = c_ref[...].astype(F32)
    c = [rows_of_step(wide, t, blocks) for t in range(steps)]
    row = lax.broadcasted_iota(jnp.int32, c[0].shape, 0)
    down = []
    up = []
    for t in range(1, HALO // 2):
        down.append(jnp.where(row >= t, c[HALO - t], pltpu.roll(c[t], t, 0)))
        up.append(jnp.where(row < HALO - t, c[HALO - t], pltpu.roll(c[t], HALO - t, 0)))
    even = is_even()
    edge = terminal_ref[...] * TERMINAL_SCALE
    first = [jnp.where(even, d, u) for d, u in zip(down, up)] + [c[HALO // 2], edge]
    second = [jnp.where(even, u, d) for d, u in zip(down, up)] + [c[HALO // 2], edge]
    first_ref[...] = to_i16(jnp.concatenate(first, axis=0))
    second_ref[...] = to_i16(jnp.concatenate(second, axis=0))


def shares(ahead):
    falling = jnp.minimum(ahead, 0.0)
    low = (time_step * viscosity) * ahead - falling * falling
    return low, ahead * ahead + low


def flux(drift, m, beyond):
    return (jnp.maximum(drift, 0.0) + KAPPA * viscosity) * (m - beyond) + drift * beyond


def backward_kernel(
    blocks, steps, w_ref, c_ref, terminal_ref, init_ref, first_ref, second_ref, u_ref, first_edge_ref, second_edge_ref, sums_ref
):
    pops = w_ref.shape[0]
    cols = terminal_ref.shape[1]
    own = lax.axis_index(POP)
    own_weights = w_ref[pl.ds(own, 1), :].astype(F32)
    total = jnp.sum(own_weights, axis=1, keepdims=True)
    size = jnp.maximum(jnp.sum(jnp.abs(own_weights), axis=1, keepdims=True), 1.0)
    slope = size * (KAPPA * time_step * DENSITY_HALF / (LEVELS * pops))
    offset = total * (KAPPA * time_step * DENSITY_MID / pops)
    wide = c_ref[...].astype(F32)
    even = is_even()
    first = first_ref[...].astype(F32)
    second = second_ref[...].astype(F32)
    above = jnp.where(even, second, first)
    below = jnp.where(even, first, second)

    def tile(x, k):
        return x[k * HALO : (k + 1) * HALO]

    def levels(t):
        if t == 0:
            top = bottom = jnp.zeros((HALO, cols), F32)
        elif t <= HALO // 2:
            top = tile(above, t - 1)
            bottom = tile(below, t - 1)
            if t < HALO // 2:
                top = pltpu.roll(top, HALO - t, 0)
                bottom = pltpu.roll(bottom, t, 0)
        else:
            top = tile(above, HALO - t - 1)
            bottom = tile(below, HALO - t - 1)
        return jnp.concatenate([top, rows_of_step(wide, t, blocks), bottom], axis=0)

    last = HALO // 2
    u = jnp.concatenate(
        [
            tile(above, last) * (KAPPA / TERMINAL_SCALE),
            terminal_ref[...] * KAPPA,
            tile(below, last) * (KAPPA / TERMINAL_SCALE),
        ],
        axis=0,
    )
    high = u.shape[0]
    partial = [None] * steps
    kept = [None] * steps
    for t in reversed(range(steps)):
        ahead_r = pltpu.roll(u, high - 1, 0) - u
        ahead_c = pltpu.roll(u, cols - 1, 1) - u
        low_r, up_r = shares(ahead_r)
        low_c, up_c = shares(ahead_c)
        source = levels(t) * slope + offset
        u = (u + source) + (low_r - pltpu.roll(up_r, 1, 0)) + (low_c - pltpu.roll(up_c, 1, 1))
        u_ref[t] = u
        mine = u[HALO : 2 * HALO]
        kept[t] = mine
        lanes = mine[:, :128]
        for k in range(1, cols // 128):
            lanes = lanes + mine[:, k * 128 : (k + 1) * 128]
        partial[t] = jnp.sum(lanes, axis=0, keepdims=True)
    sums = jnp.sum(jnp.concatenate(partial, axis=0), axis=1, keepdims=True)
    lane = lax.broadcasted_iota(jnp.int32, (steps, 128), 1)
    step = lax.broadcasted_iota(jnp.int32, (steps, 128), 0)
    line = jnp.sum(jnp.where(lane == step, sums, 0.0), axis=0, keepdims=True)
    sums_ref[...] = jnp.broadcast_to(
        jnp.concatenate([line] * (sums_ref.shape[2] // 128), axis=1)[None], sums_ref.shape
    )
    row = lax.broadcasted_iota(jnp.int32, (HALO, cols), 0)
    largest = jnp.maximum(
        jnp.maximum(jnp.abs(kept[0]), jnp.abs(kept[1])),
        jnp.maximum(jnp.abs(kept[2]), jnp.abs(kept[3])),
    )
    largest = jnp.max(jnp.max(largest, axis=1, keepdims=True), axis=0, keepdims=True)
    exponent = jnp.ceil(jnp.log2(jnp.maximum(largest, 1e-30)))
    scale = LEVELS / jnp.exp2(exponent)
    inner = jnp.where((row >= 1) & (row <= 6), kept[1], pltpu.roll(kept[3], 4, 0))
    first_edge_ref[0:8] = init_ref[...]
    first_edge_ref[8:16] = kept[0]
    first_edge_ref[16:24] = inner
    first_edge_ref[24:32] = kept[2]
    second_edge_ref[...] = to_i16(
        jnp.concatenate(
            [
                (init_ref[...] - INIT_MID) * INIT_SCALE,
                kept[0] * scale,
                inner * scale,
                jnp.where(row == 0, exponent, kept[2] * scale),
            ],
            axis=0,
        )
    )


def decoded(edge):
    edge = edge.astype(F32)
    size = jnp.exp2(edge[24:25, 0:1]) * (1.0 / LEVELS)
    return jnp.concatenate([edge[0:8] * (1.0 / INIT_SCALE) + INIT_MID, edge[8:32] * size], axis=0)


def forward_kernel(
    cells, steps, u_ref, init_ref, second_ref, first_ref, sums_ref, values_ref, final_ref
):
    cols = init_ref.shape[1]
    row = lax.broadcasted_iota(jnp.int32, (HALO, cols), 0)
    even = is_even()
    first = first_ref[...]
    second = decoded(second_ref[...])
    above = jnp.where(even, second, first)
    below = jnp.where(even, first, second)
    m = jnp.concatenate([above[0:8], init_ref[...], below[0:8]], axis=0)
    high = m.shape[0]

    def field(t):
        u = u_ref[t]
        if t > 3:
            return u

        def side(far, near):
            if t == 0:
                return far[8:16]
            if t == 1:
                return jnp.where((row >= 1) & (row <= 6), far[16:24], near)
            if t == 2:
                return jnp.where((row >= 2) & (row <= 5), far[24:32], near)
            return jnp.where((row >= 3) & (row <= 4), pltpu.roll(far[16:24], 4, 0), near)

        return jnp.concatenate(
            [side(above, u[0:8]), u[8:16], side(below, u[16:24])], axis=0
        )

    means = jnp.sum(sums_ref[:, :, 0:128], axis=0) * (1.0 / cells)
    for t in range(steps):
        values_ref[t] = (u_ref[t, HALO : 2 * HALO, :] - means[:, t : t + 1]) * (1.0 / KAPPA)
        u = field(t)
        down_m = pltpu.roll(m, high - 1, 0)
        right_m = pltpu.roll(m, cols - 1, 1)
        flux_r = flux(u - pltpu.roll(u, high - 1, 0), m, down_m)
        flux_c = flux(u - pltpu.roll(u, cols - 1, 1), m, right_m)
        m = m - (time_step / KAPPA) * (
            (flux_r - pltpu.roll(flux_r, 1, 0)) + (flux_c - pltpu.roll(flux_c, 1, 1))
        )
    final_ref[...] = m[HALO : 2 * HALO]


def call(kernel, outs, *args):
    spec = pl.BlockSpec(memory_space=pltpu.VMEM)
    return pl.pallas_call(
        kernel,
        out_shape=outs,
        in_specs=[spec] * len(args),
        out_specs=jax.tree.map(lambda _: spec, outs),
        compiler_params=pltpu.CompilerParams(vmem_limit_bytes=40 * 1024 * 1024),
    )(*args)


def first_swap(x):
    peers = lax.axis_size("tile")
    return lax.ppermute(x, "tile", [(i, i ^ 1) for i in range(peers)])


def second_swap(x):
    peers = lax.axis_size("tile")
    return lax.ppermute(x, "tile", [(i, (((i + 1) ^ 1) - 1) % peers) for i in range(peers)])


def per_device(weights, terminal, density_history, density_init):
    pops = weights.shape[0]
    steps, rows, cols = density_history.shape[1:]
    tiles = lax.axis_size("tile")
    blocks = pops // steps
    part = cols // blocks
    struct = jax.ShapeDtypeStruct
    terminal = terminal[0]
    init = density_init[0]
    chunks = density_history[0].reshape(steps, rows, blocks, part).transpose(0, 2, 1, 3)
    chunks = lax.all_to_all(chunks.reshape(pops, rows, part), POP, 0, 0, tiled=True)
    kron, scale = call(
        spread_kernel,
        (struct((pops * rows, pops * rows), jnp.bfloat16), struct((pops * rows, 128), F32)),
        weights,
    )
    levels = call(
        coupling_kernel,
        struct((pops * rows, part), I16),
        kron,
        scale,
        chunks.reshape(pops * rows, part),
    )
    levels = lax.all_to_all(levels.reshape(pops, rows, part), POP, 0, 0, tiled=True)
    levels = levels.reshape(pops * rows, part)
    first, second = call(
        functools.partial(pack_kernel, blocks, steps),
        (struct((40, cols), I16), struct((40, cols), I16)),
        levels,
        terminal,
    )
    second = second_swap(second)
    first = first_swap(first)
    fields, first, second, sums = call(
        functools.partial(backward_kernel, blocks, steps),
        (
            struct((steps, 3 * HALO, cols), F32),
            struct((32, cols), F32),
            struct((32, cols), I16),
            struct((tiles, 1, 1152), F32),
        ),
        weights,
        levels,
        terminal,
        init,
        first,
        second,
    )
    first = first_swap(first)
    second = second_swap(second)
    sums = lax.all_to_all(sums, "tile", 0, 0, tiled=True)
    values, final = call(
        functools.partial(forward_kernel, float(tiles * rows * cols), steps),
        (struct((steps, rows, cols), F32), struct((rows, cols), F32)),
        fields,
        init,
        second,
        first,
        sums,
    )
    return values[None], final[None]


def solution(mesh):
    split = Mesh(
        mesh.devices.reshape(8, 2, 2, mesh.shape["tile"]), ("pop_0", "pop_1", "pop_2", "tile")
    )
    in_specs = (P(), P(POP, "tile", None), P(POP, None, "tile", None), P(POP, "tile", None))
    out_specs = (P(POP, None, "tile", None), P(POP, "tile", None))
    return jax.shard_map(
        per_device, mesh=split, in_specs=in_specs, out_specs=out_specs, check_vma=False
    )
```

```python
import functools

import jax
import jax.numpy as jnp
from jax import lax
from jax.experimental import pallas as pl
from jax.experimental.pallas import tpu as pltpu
from jax.sharding import Mesh
from jax.sharding import PartitionSpec as P

POP = ("pop_0", "pop_1", "pop_2")

time_step = 0.2
viscosity = 0.2

DENSITY_MID = (0.19921875 + 2.0) / 2
DENSITY_HALF = (2.0 - 0.19921875) / 2
LEVELS = 32000.0
TERMINAL_SCALE = 32000.0 / 4.5
INIT_MID = 1.1
INIT_SCALE = 32000.0 / 0.9

HALO = 8
KAPPA = time_step / 2

F32 = jnp.float32
I16 = jnp.int16


def to_i16(x):
    return jnp.round(x).astype(jnp.int32).astype(I16)


def spread_kernel(w_ref, kron_ref, scale_ref):
    pops = w_ref.shape[0]
    rows = kron_ref.shape[0]
    per = rows // pops
    shift = per.bit_length() - 1
    weights = w_ref[...].astype(F32).astype(jnp.bfloat16)
    i = lax.broadcasted_iota(jnp.int32, (rows, pops), 0)
    q = lax.broadcasted_iota(jnp.int32, (rows, pops), 1)
    spread = jnp.where((i >> shift) == q, 1.0, 0.0).astype(jnp.bfloat16)
    tall = jnp.dot(spread, weights, preferred_element_type=F32)
    total = jnp.sum(tall, axis=1, keepdims=True)
    size = jnp.maximum(jnp.sum(jnp.abs(tall), axis=1, keepdims=True), 1.0)
    wide = lax.dot_general(
        tall.astype(jnp.bfloat16), spread, (((1,), (1,)), ((), ())), preferred_element_type=F32
    )
    a = lax.broadcasted_iota(jnp.int32, (rows, rows), 0)
    b = lax.broadcasted_iota(jnp.int32, (rows, rows), 1)
    kron_ref[...] = jnp.where((a & (per - 1)) == (b & (per - 1)), wide, 0.0).astype(jnp.bfloat16)
    lane = lax.broadcasted_iota(jnp.int32, scale_ref.shape, 1)
    scale_ref[...] = jnp.where(
        lane == 0, DENSITY_MID * total, LEVELS / (DENSITY_HALF * size)
    )


def coupling_kernel(kron_ref, scale_ref, x_ref, out_ref):
    product = jnp.dot(kron_ref[...], x_ref[...], preferred_element_type=F32)
    out_ref[...] = to_i16((product - scale_ref[:, 0:1]) * scale_ref[:, 1:2])


def rows_of_step(wide, step, blocks):
    first = step * blocks * HALO
    return jnp.concatenate(
        [wide[first + k * HALO : first + (k + 1) * HALO] for k in range(blocks)], axis=1
    )


def is_even():
    return (lax.axis_index("tile") & 1) == 0


def pack_kernel(blocks, steps, c_ref, terminal_ref, first_ref, second_ref):
    wide = c_ref[...].astype(F32)
    c = [rows_of_step(wide, t, blocks) for t in range(steps)]
    row = lax.broadcasted_iota(jnp.int32, c[0].shape, 0)
    down = []
    up = []
    for t in range(1, HALO // 2):
        down.append(jnp.where(row >= t, c[HALO - t], pltpu.roll(c[t], t, 0)))
        up.append(jnp.where(row < HALO - t, c[HALO - t], pltpu.roll(c[t], HALO - t, 0)))
    even = is_even()
    edge = terminal_ref[...] * TERMINAL_SCALE
    half = edge.shape[1] // 2
    left, right = c[HALO // 2][:, :half], pltpu.roll(c[HALO // 2][:, half:], HALO // 2, 0)
    upper = row[:, :half] < HALO // 2
    down_mid = jnp.where(upper, right, left)
    up_mid = jnp.where(upper, left, right)

    def stacked(tiles, mid):
        parts = [x[:, at : at + half] for x in tiles + [edge] for at in (0, half)]
        return to_i16(jnp.concatenate(parts + [mid], axis=0))

    first = [jnp.where(even, d, u) for d, u in zip(down, up)]
    second = [jnp.where(even, u, d) for d, u in zip(down, up)]
    first_ref[...] = stacked(first, jnp.where(even, down_mid, up_mid))
    second_ref[...] = stacked(second, jnp.where(even, up_mid, down_mid))


def shares(ahead):
    falling = jnp.minimum(ahead, 0.0)
    low = (time_step * viscosity) * ahead - falling * falling
    return low, ahead * ahead + low


def flux(drift, m, beyond):
    return (jnp.maximum(drift, 0.0) + KAPPA * viscosity) * (m - beyond) + drift * beyond


def backward_kernel(
    blocks, steps, w_ref, c_ref, terminal_ref, init_ref, first_ref, second_ref, u_ref, first_edge_ref, second_edge_ref, sums_ref
):
    pops = w_ref.shape[0]
    cols = terminal_ref.shape[1]
    own = lax.axis_index(POP)
    own_weights = w_ref[pl.ds(own, 1), :].astype(F32)
    total = jnp.sum(own_weights, axis=1, keepdims=True)
    size = jnp.maximum(jnp.sum(jnp.abs(own_weights), axis=1, keepdims=True), 1.0)
    slope = size * (KAPPA * time_step * DENSITY_HALF / (LEVELS * pops))
    offset = total * (KAPPA * time_step * DENSITY_MID / pops)
    wide = c_ref[...].astype(F32)
    even = is_even()
    first = first_ref[...].astype(F32)
    second = second_ref[...].astype(F32)
    above = jnp.where(even, second, first)
    below = jnp.where(even, first, second)

    def tile(x, k):
        at = 2 * k * HALO
        return jnp.concatenate([x[at : at + HALO], x[at + HALO : at + 2 * HALO]], axis=1)

    def middle(x):
        shared = x[HALO * HALO :]
        return jnp.concatenate([shared, pltpu.roll(shared, HALO // 2, 0)], axis=1)

    def levels(t):
        if t == 0:
            top = bottom = jnp.zeros((HALO, cols), F32)
        elif t < HALO // 2:
            top = pltpu.roll(tile(above, t - 1), HALO - t, 0)
            bottom = pltpu.roll(tile(below, t - 1), t, 0)
        elif t == HALO // 2:
            top = middle(above)
            bottom = middle(below)
        else:
            top = tile(above, HALO - t - 1)
            bottom = tile(below, HALO - t - 1)
        return jnp.concatenate([top, rows_of_step(wide, t, blocks), bottom], axis=0)

    last = HALO // 2 - 1
    u = jnp.concatenate(
        [
            tile(above, last) * (KAPPA / TERMINAL_SCALE),
            terminal_ref[...] * KAPPA,
            tile(below, last) * (KAPPA / TERMINAL_SCALE),
        ],
        axis=0,
    )
    high = u.shape[0]
    partial = [None] * steps
    kept = [None] * steps
    for t in reversed(range(steps)):
        ahead_r = pltpu.roll(u, high - 1, 0) - u
        ahead_c = pltpu.roll(u, cols - 1, 1) - u
        low_r, up_r = shares(ahead_r)
        low_c, up_c = shares(ahead_c)
        source = levels(t) * slope + offset
        u = (u + source) + (low_r - pltpu.roll(up_r, 1, 0)) + (low_c - pltpu.roll(up_c, 1, 1))
        u_ref[t] = u
        mine = u[HALO : 2 * HALO]
        kept[t] = mine
        lanes = mine[:, :128]
        for k in range(1, cols // 128):
            lanes = lanes + mine[:, k * 128 : (k + 1) * 128]
        partial[t] = jnp.sum(lanes, axis=0, keepdims=True)
    sums = jnp.sum(jnp.concatenate(partial, axis=0), axis=1, keepdims=True)
    lane = lax.broadcasted_iota(jnp.int32, (steps, 128), 1)
    step = lax.broadcasted_iota(jnp.int32, (steps, 128), 0)
    line = jnp.sum(jnp.where(lane == step, sums, 0.0), axis=0, keepdims=True)
    sums_ref[...] = jnp.broadcast_to(
        jnp.concatenate([line] * (sums_ref.shape[2] // 128), axis=1)[None], sums_ref.shape
    )
    row = lax.broadcasted_iota(jnp.int32, (HALO, cols), 0)
    largest = jnp.maximum(
        jnp.maximum(jnp.abs(kept[0]), jnp.abs(kept[1])),
        jnp.maximum(jnp.abs(kept[2]), jnp.abs(kept[3])),
    )
    largest = jnp.max(jnp.max(largest, axis=1, keepdims=True), axis=0, keepdims=True)
    exponent = jnp.ceil(jnp.log2(jnp.maximum(largest, 1e-30)))
    scale = LEVELS / jnp.exp2(exponent)
    inner = jnp.where((row >= 1) & (row <= 6), kept[1], pltpu.roll(kept[3], 4, 0))
    first_edge_ref[0:8] = init_ref[...]
    first_edge_ref[8:16] = kept[0]
    first_edge_ref[16:24] = inner
    first_edge_ref[24:32] = kept[2]
    second_edge_ref[...] = to_i16(
        jnp.concatenate(
            [
                (init_ref[...] - INIT_MID) * INIT_SCALE,
                kept[0] * scale,
                inner * scale,
                jnp.where(row == 0, exponent, kept[2] * scale),
            ],
            axis=0,
        )
    )


def decoded(edge):
    edge = edge.astype(F32)
    size = jnp.exp2(edge[24:25, 0:1]) * (1.0 / LEVELS)
    return jnp.concatenate([edge[0:8] * (1.0 / INIT_SCALE) + INIT_MID, edge[8:32] * size], axis=0)


def forward_kernel(
    cells, steps, u_ref, init_ref, second_ref, first_ref, sums_ref, values_ref, final_ref
):
    cols = init_ref.shape[1]
    row = lax.broadcasted_iota(jnp.int32, (HALO, cols), 0)
    even = is_even()
    first = first_ref[...]
    second = decoded(second_ref[...])
    above = jnp.where(even, second, first)
    below = jnp.where(even, first, second)
    m = jnp.concatenate([above[0:8], init_ref[...], below[0:8]], axis=0)
    high = m.shape[0]

    def field(t):
        u = u_ref[t]
        if t > 3:
            return u

        def side(far, near):
            if t == 0:
                return far[8:16]
            if t == 1:
                return jnp.where((row >= 1) & (row <= 6), far[16:24], near)
            if t == 2:
                return jnp.where((row >= 2) & (row <= 5), far[24:32], near)
            return jnp.where((row >= 3) & (row <= 4), pltpu.roll(far[16:24], 4, 0), near)

        return jnp.concatenate(
            [side(above, u[0:8]), u[8:16], side(below, u[16:24])], axis=0
        )

    means = jnp.sum(sums_ref[:, :, 0:128], axis=0) * (1.0 / cells)
    for t in range(steps):
        values_ref[t] = (u_ref[t, HALO : 2 * HALO, :] - means[:, t : t + 1]) * (1.0 / KAPPA)
        u = field(t)
        down_m = pltpu.roll(m, high - 1, 0)
        right_m = pltpu.roll(m, cols - 1, 1)
        flux_r = flux(u - pltpu.roll(u, high - 1, 0), m, down_m)
        flux_c = flux(u - pltpu.roll(u, cols - 1, 1), m, right_m)
        m = m - (time_step / KAPPA) * (
            (flux_r - pltpu.roll(flux_r, 1, 0)) + (flux_c - pltpu.roll(flux_c, 1, 1))
        )
    final_ref[...] = m[HALO : 2 * HALO]


def call(kernel, outs, *args):
    spec = pl.BlockSpec(memory_space=pltpu.VMEM)
    return pl.pallas_call(
        kernel,
        out_shape=outs,
        in_specs=[spec] * len(args),
        out_specs=jax.tree.map(lambda _: spec, outs),
        compiler_params=pltpu.CompilerParams(vmem_limit_bytes=40 * 1024 * 1024),
    )(*args)


def first_swap(x):
    peers = lax.axis_size("tile")
    return lax.ppermute(x, "tile", [(i, i ^ 1) for i in range(peers)])


def second_swap(x):
    peers = lax.axis_size("tile")
    return lax.ppermute(x, "tile", [(i, (((i + 1) ^ 1) - 1) % peers) for i in range(peers)])


def per_device(weights, terminal, density_history, density_init):
    pops = weights.shape[0]
    steps, rows, cols = density_history.shape[1:]
    tiles = lax.axis_size("tile")
    blocks = pops // steps
    part = cols // blocks
    struct = jax.ShapeDtypeStruct
    terminal = terminal[0]
    init = density_init[0]
    chunks = density_history[0].reshape(steps, rows, blocks, part).transpose(0, 2, 1, 3)
    chunks = lax.all_to_all(chunks.reshape(pops, rows, part), POP, 0, 0, tiled=True)
    kron, scale = call(
        spread_kernel,
        (struct((pops * rows, pops * rows), jnp.bfloat16), struct((pops * rows, 128), F32)),
        weights,
    )
    levels = call(
        coupling_kernel,
        struct((pops * rows, part), I16),
        kron,
        scale,
        chunks.reshape(pops * rows, part),
    )
    levels = lax.all_to_all(levels.reshape(pops, rows, part), POP, 0, 0, tiled=True)
    levels = levels.reshape(pops * rows, part)
    first, second = call(
        functools.partial(pack_kernel, blocks, steps),
        (struct((72, cols // 2), I16), struct((72, cols // 2), I16)),
        levels,
        terminal,
    )
    second = second_swap(second)
    first = first_swap(first)
    fields, first, second, sums = call(
        functools.partial(backward_kernel, blocks, steps),
        (
            struct((steps, 3 * HALO, cols), F32),
            struct((32, cols), F32),
            struct((32, cols), I16),
            struct((tiles, 1, 1152), F32),
        ),
        weights,
        levels,
        terminal,
        init,
        first,
        second,
    )
    first = first_swap(first)
    second = second_swap(second)
    sums = lax.all_to_all(sums, "tile", 0, 0, tiled=True)
    values, final = call(
        functools.partial(forward_kernel, float(tiles * rows * cols), steps),
        (struct((steps, rows, cols), F32), struct((rows, cols), F32)),
        fields,
        init,
        second,
        first,
        sums,
    )
    return values[None], final[None]


def solution(mesh):
    split = Mesh(
        mesh.devices.reshape(8, 2, 2, mesh.shape["tile"]), ("pop_0", "pop_1", "pop_2", "tile")
    )
    in_specs = (P(), P(POP, "tile", None), P(POP, None, "tile", None), P(POP, "tile", None))
    out_specs = (P(POP, None, "tile", None), P(POP, "tile", None))
    return jax.shard_map(
        per_device, mesh=split, in_specs=in_specs, out_specs=out_specs, check_vma=False
    )
```

```python
import functools

import jax
import jax.numpy as jnp
from jax import lax
from jax.experimental import pallas as pl
from jax.experimental.pallas import tpu as pltpu
from jax.sharding import Mesh
from jax.sharding import PartitionSpec as P

POP = ("pop_0", "pop_1", "pop_2")

time_step = 0.2
viscosity = 0.2

DENSITY_MID = (0.19921875 + 2.0) / 2
DENSITY_HALF = (2.0 - 0.19921875) / 2
LEVELS = 32000.0
TERMINAL_SCALE = 32000.0 / 4.5
INIT_MID = 1.1
INIT_SCALE = 32000.0 / 0.9

HALO = 8
KAPPA = time_step / 2

F32 = jnp.float32
I16 = jnp.int16


def to_i16(x):
    return jnp.round(x).astype(jnp.int32).astype(I16)


def spread_kernel(w_ref, terminal_ref, kron_ref, scale_ref, rim_ref):
    rim_ref[...] = to_i16(terminal_ref[...] * TERMINAL_SCALE)
    pops = w_ref.shape[0]
    rows = kron_ref.shape[0]
    per = rows // pops
    shift = per.bit_length() - 1
    weights = w_ref[...].astype(F32).astype(jnp.bfloat16)
    i = lax.broadcasted_iota(jnp.int32, (rows, pops), 0)
    q = lax.broadcasted_iota(jnp.int32, (rows, pops), 1)
    spread = jnp.where((i >> shift) == q, 1.0, 0.0).astype(jnp.bfloat16)
    tall = jnp.dot(spread, weights, preferred_element_type=F32)
    total = jnp.sum(tall, axis=1, keepdims=True)
    size = jnp.maximum(jnp.sum(jnp.abs(tall), axis=1, keepdims=True), 1.0)
    wide = lax.dot_general(
        tall.astype(jnp.bfloat16), spread, (((1,), (1,)), ((), ())), preferred_element_type=F32
    )
    a = lax.broadcasted_iota(jnp.int32, (rows, rows), 0)
    b = lax.broadcasted_iota(jnp.int32, (rows, rows), 1)
    kron_ref[...] = jnp.where((a & (per - 1)) == (b & (per - 1)), wide, 0.0).astype(jnp.bfloat16)
    lane = lax.broadcasted_iota(jnp.int32, scale_ref.shape, 1)
    scale_ref[...] = jnp.where(
        lane == 0, DENSITY_MID * total, LEVELS / (DENSITY_HALF * size)
    )


def coupling_kernel(kron_ref, scale_ref, x_ref, out_ref):
    product = jnp.dot(kron_ref[...], x_ref[...], preferred_element_type=F32)
    out_ref[...] = to_i16((product - scale_ref[:, 0:1]) * scale_ref[:, 1:2])


def rows_of_step(wide, step, blocks):
    first = step * blocks * HALO
    return jnp.concatenate(
        [wide[first + k * HALO : first + (k + 1) * HALO] for k in range(blocks)], axis=1
    )


def is_even():
    return (lax.axis_index("tile") & 1) == 0


def pack_kernel(blocks, steps, c_ref, first_ref, second_ref):
    wide = c_ref[...].astype(F32)
    c = [rows_of_step(wide, t, blocks) for t in range(steps)]
    row = lax.broadcasted_iota(jnp.int32, c[0].shape, 0)
    down = []
    up = []
    for t in range(1, HALO // 2):
        down.append(jnp.where(row >= t, c[HALO - t], pltpu.roll(c[t], t, 0)))
        up.append(jnp.where(row < HALO - t, c[HALO - t], pltpu.roll(c[t], HALO - t, 0)))
    even = is_even()
    half = row.shape[1] // 2
    left, right = c[HALO // 2][:, :half], pltpu.roll(c[HALO // 2][:, half:], HALO // 2, 0)
    upper = row[:, :half] < HALO // 2
    down_mid = jnp.where(upper, right, left)
    up_mid = jnp.where(upper, left, right)

    def stacked(tiles, mid):
        parts = [x[:, at : at + half] for x in tiles for at in (0, half)]
        return to_i16(jnp.concatenate(parts + [mid], axis=0))

    first = [jnp.where(even, d, u) for d, u in zip(down, up)]
    second = [jnp.where(even, u, d) for d, u in zip(down, up)]
    first_ref[...] = stacked(first, jnp.where(even, down_mid, up_mid))
    second_ref[...] = stacked(second, jnp.where(even, up_mid, down_mid))


def shares(ahead):
    falling = jnp.minimum(ahead, 0.0)
    low = (time_step * viscosity) * ahead - falling * falling
    return low, ahead * ahead + low


def flux(drift, m, beyond):
    return (jnp.maximum(drift, 0.0) + KAPPA * viscosity) * (m - beyond) + drift * beyond


def backward_kernel(
    blocks, steps, w_ref, c_ref, terminal_ref, init_ref, first_rim_ref, second_rim_ref, first_ref, second_ref, u_ref, first_edge_ref, second_edge_ref, sums_ref
):
    pops = w_ref.shape[0]
    cols = terminal_ref.shape[1]
    own = lax.axis_index(POP)
    own_weights = w_ref[pl.ds(own, 1), :].astype(F32)
    total = jnp.sum(own_weights, axis=1, keepdims=True)
    size = jnp.maximum(jnp.sum(jnp.abs(own_weights), axis=1, keepdims=True), 1.0)
    slope = size * (KAPPA * time_step * DENSITY_HALF / (LEVELS * pops))
    offset = total * (KAPPA * time_step * DENSITY_MID / pops)
    wide = c_ref[...].astype(F32)
    even = is_even()
    first = first_ref[...].astype(F32)
    second = second_ref[...].astype(F32)
    above = jnp.where(even, second, first)
    below = jnp.where(even, first, second)

    def tile(x, k):
        at = 2 * k * HALO
        return jnp.concatenate([x[at : at + HALO], x[at + HALO : at + 2 * HALO]], axis=1)

    def middle(x):
        shared = x[HALO * (HALO - 2) :]
        return jnp.concatenate([shared, pltpu.roll(shared, HALO // 2, 0)], axis=1)

    def levels(t):
        if t == 0:
            top = bottom = jnp.zeros((HALO, cols), F32)
        elif t < HALO // 2:
            top = pltpu.roll(tile(above, t - 1), HALO - t, 0)
            bottom = pltpu.roll(tile(below, t - 1), t, 0)
        elif t == HALO // 2:
            top = middle(above)
            bottom = middle(below)
        else:
            top = tile(above, HALO - t - 1)
            bottom = tile(below, HALO - t - 1)
        return jnp.concatenate([top, rows_of_step(wide, t, blocks), bottom], axis=0)

    first_rim = first_rim_ref[...].astype(F32) * (KAPPA / TERMINAL_SCALE)
    second_rim = second_rim_ref[...].astype(F32) * (KAPPA / TERMINAL_SCALE)
    u = jnp.concatenate(
        [
            jnp.where(even, second_rim, first_rim),
            terminal_ref[...] * KAPPA,
            jnp.where(even, first_rim, second_rim),
        ],
        axis=0,
    )
    high = u.shape[0]
    partial = [None] * steps
    kept = [None] * steps
    for t in reversed(range(steps)):
        ahead_r = pltpu.roll(u, high - 1, 0) - u
        ahead_c = pltpu.roll(u, cols - 1, 1) - u
        low_r, up_r = shares(ahead_r)
        low_c, up_c = shares(ahead_c)
        source = levels(t) * slope + offset
        u = (u + source) + (low_r - pltpu.roll(up_r, 1, 0)) + (low_c - pltpu.roll(up_c, 1, 1))
        u_ref[t] = u
        mine = u[HALO : 2 * HALO]
        kept[t] = mine
        lanes = mine[:, :128]
        for k in range(1, cols // 128):
            lanes = lanes + mine[:, k * 128 : (k + 1) * 128]
        partial[t] = jnp.sum(lanes, axis=0, keepdims=True)
    sums = jnp.sum(jnp.concatenate(partial, axis=0), axis=1, keepdims=True)
    lane = lax.broadcasted_iota(jnp.int32, (steps, 128), 1)
    step = lax.broadcasted_iota(jnp.int32, (steps, 128), 0)
    line = jnp.sum(jnp.where(lane == step, sums, 0.0), axis=0, keepdims=True)
    sums_ref[...] = jnp.broadcast_to(
        jnp.concatenate([line] * (sums_ref.shape[2] // 128), axis=1)[None], sums_ref.shape
    )
    row = lax.broadcasted_iota(jnp.int32, (HALO, cols), 0)
    largest = jnp.maximum(
        jnp.maximum(jnp.abs(kept[0]), jnp.abs(kept[1])),
        jnp.maximum(jnp.abs(kept[2]), jnp.abs(kept[3])),
    )
    largest = jnp.max(jnp.max(largest, axis=1, keepdims=True), axis=0, keepdims=True)
    exponent = jnp.ceil(jnp.log2(jnp.maximum(largest, 1e-30)))
    scale = LEVELS / jnp.exp2(exponent)
    inner = jnp.where((row >= 1) & (row <= 6), kept[1], pltpu.roll(kept[3], 4, 0))
    first_edge_ref[0:8] = init_ref[...]
    first_edge_ref[8:16] = kept[0]
    first_edge_ref[16:24] = inner
    first_edge_ref[24:32] = kept[2]
    second_edge_ref[...] = to_i16(
        jnp.concatenate(
            [
                (init_ref[...] - INIT_MID) * INIT_SCALE,
                kept[0] * scale,
                inner * scale,
                jnp.where(row == 0, exponent, kept[2] * scale),
            ],
            axis=0,
        )
    )


def decoded(edge):
    edge = edge.astype(F32)
    size = jnp.exp2(edge[24:25, 0:1]) * (1.0 / LEVELS)
    return jnp.concatenate([edge[0:8] * (1.0 / INIT_SCALE) + INIT_MID, edge[8:32] * size], axis=0)


def forward_kernel(
    cells, steps, u_ref, init_ref, second_ref, first_ref, sums_ref, values_ref, final_ref
):
    cols = init_ref.shape[1]
    row = lax.broadcasted_iota(jnp.int32, (HALO, cols), 0)
    even = is_even()
    first = first_ref[...]
    second = decoded(second_ref[...])
    above = jnp.where(even, second, first)
    below = jnp.where(even, first, second)
    m = jnp.concatenate([above[0:8], init_ref[...], below[0:8]], axis=0)
    high = m.shape[0]

    def field(t):
        u = u_ref[t]
        if t > 3:
            return u

        def side(far, near):
            if t == 0:
                return far[8:16]
            if t == 1:
                return jnp.where((row >= 1) & (row <= 6), far[16:24], near)
            if t == 2:
                return jnp.where((row >= 2) & (row <= 5), far[24:32], near)
            return jnp.where((row >= 3) & (row <= 4), pltpu.roll(far[16:24], 4, 0), near)

        return jnp.concatenate(
            [side(above, u[0:8]), u[8:16], side(below, u[16:24])], axis=0
        )

    means = jnp.sum(sums_ref[:, :, 0:128], axis=0) * (1.0 / cells)
    for t in range(steps):
        values_ref[t] = (u_ref[t, HALO : 2 * HALO, :] - means[:, t : t + 1]) * (1.0 / KAPPA)
        u = field(t)
        down_m = pltpu.roll(m, high - 1, 0)
        right_m = pltpu.roll(m, cols - 1, 1)
        flux_r = flux(u - pltpu.roll(u, high - 1, 0), m, down_m)
        flux_c = flux(u - pltpu.roll(u, cols - 1, 1), m, right_m)
        m = m - (time_step / KAPPA) * (
            (flux_r - pltpu.roll(flux_r, 1, 0)) + (flux_c - pltpu.roll(flux_c, 1, 1))
        )
    final_ref[...] = m[HALO : 2 * HALO]


def call(kernel, outs, *args):
    spec = pl.BlockSpec(memory_space=pltpu.VMEM)
    return pl.pallas_call(
        kernel,
        out_shape=outs,
        in_specs=[spec] * len(args),
        out_specs=jax.tree.map(lambda _: spec, outs),
        compiler_params=pltpu.CompilerParams(vmem_limit_bytes=40 * 1024 * 1024),
    )(*args)


def first_swap(x):
    peers = lax.axis_size("tile")
    return lax.ppermute(x, "tile", [(i, i ^ 1) for i in range(peers)])


def second_swap(x):
    peers = lax.axis_size("tile")
    return lax.ppermute(x, "tile", [(i, (((i + 1) ^ 1) - 1) % peers) for i in range(peers)])


def per_device(weights, terminal, density_history, density_init):
    pops = weights.shape[0]
    steps, rows, cols = density_history.shape[1:]
    tiles = lax.axis_size("tile")
    blocks = pops // steps
    part = cols // blocks
    struct = jax.ShapeDtypeStruct
    terminal = terminal[0]
    init = density_init[0]
    chunks = density_history[0].reshape(steps, rows, blocks, part).transpose(0, 2, 1, 3)
    chunks = lax.all_to_all(chunks.reshape(pops, rows, part), POP, 0, 0, tiled=True)
    kron, scale, rim = call(
        spread_kernel,
        (
            struct((pops * rows, pops * rows), jnp.bfloat16),
            struct((pops * rows, 128), F32),
            struct((rows, cols), I16),
        ),
        weights,
        terminal,
    )
    first_rim = first_swap(rim)
    second_rim = second_swap(rim)
    chunks, first_rim, second_rim = lax.optimization_barrier((chunks, first_rim, second_rim))
    levels = call(
        coupling_kernel,
        struct((pops * rows, part), I16),
        kron,
        scale,
        chunks.reshape(pops * rows, part),
    )
    levels = lax.all_to_all(levels.reshape(pops, rows, part), POP, 0, 0, tiled=True)
    levels = levels.reshape(pops * rows, part)
    first, second = call(
        functools.partial(pack_kernel, blocks, steps),
        (struct((56, cols // 2), I16), struct((56, cols // 2), I16)),
        levels,
    )
    second = second_swap(second)
    first = first_swap(first)
    fields, first, second, sums = call(
        functools.partial(backward_kernel, blocks, steps),
        (
            struct((steps, 3 * HALO, cols), F32),
            struct((32, cols), F32),
            struct((32, cols), I16),
            struct((tiles, 1, 1152), F32),
        ),
        weights,
        levels,
        terminal,
        init,
        first_rim,
        second_rim,
        first,
        second,
    )
    first = first_swap(first)
    second = second_swap(second)
    sums = lax.all_to_all(sums, "tile", 0, 0, tiled=True)
    values, final = call(
        functools.partial(forward_kernel, float(tiles * rows * cols), steps),
        (struct((steps, rows, cols), F32), struct((rows, cols), F32)),
        fields,
        init,
        second,
        first,
        sums,
    )
    return values[None], final[None]


def solution(mesh):
    split = Mesh(
        mesh.devices.reshape(8, 2, 2, mesh.shape["tile"]), ("pop_0", "pop_1", "pop_2", "tile")
    )
    in_specs = (P(), P(POP, "tile", None), P(POP, None, "tile", None), P(POP, "tile", None))
    out_specs = (P(POP, None, "tile", None), P(POP, "tile", None))
    return jax.shard_map(
        per_device, mesh=split, in_specs=in_specs, out_specs=out_specs, check_vma=False
    )
```

```python
import functools

import jax
import jax.numpy as jnp
from jax import lax
from jax.experimental import pallas as pl
from jax.experimental.pallas import tpu as pltpu
from jax.sharding import Mesh
from jax.sharding import PartitionSpec as P

POP = ("pop_0", "pop_1", "pop_2")

time_step = 0.2
viscosity = 0.2

DENSITY_MID = (0.19921875 + 2.0) / 2
DENSITY_HALF = (2.0 - 0.19921875) / 2
LEVELS = 32000.0
TERMINAL_SCALE = 32000.0 / 4.5
INIT_MID = 1.1
INIT_SCALE = 32000.0 / 0.9

HALO = 8
KAPPA = time_step / 2

F32 = jnp.float32
I16 = jnp.int16


def to_i16(x):
    return jnp.round(x).astype(jnp.int32).astype(I16)


def spread_kernel(w_ref, kron_ref, scale_ref):
    pops = w_ref.shape[0]
    rows = kron_ref.shape[0]
    per = rows // pops
    shift = per.bit_length() - 1
    weights = w_ref[...].astype(F32).astype(jnp.bfloat16)
    i = lax.broadcasted_iota(jnp.int32, (rows, pops), 0)
    q = lax.broadcasted_iota(jnp.int32, (rows, pops), 1)
    spread = jnp.where((i >> shift) == q, 1.0, 0.0).astype(jnp.bfloat16)
    tall = jnp.dot(spread, weights, preferred_element_type=F32)
    total = jnp.sum(tall, axis=1, keepdims=True)
    size = jnp.maximum(jnp.sum(jnp.abs(tall), axis=1, keepdims=True), 1.0)
    wide = lax.dot_general(
        tall.astype(jnp.bfloat16), spread, (((1,), (1,)), ((), ())), preferred_element_type=F32
    )
    a = lax.broadcasted_iota(jnp.int32, (rows, rows), 0)
    b = lax.broadcasted_iota(jnp.int32, (rows, rows), 1)
    kron_ref[...] = jnp.where((a & (per - 1)) == (b & (per - 1)), wide, 0.0).astype(jnp.bfloat16)
    lane = lax.broadcasted_iota(jnp.int32, scale_ref.shape, 1)
    scale_ref[...] = jnp.where(
        lane == 0, DENSITY_MID * total, LEVELS / (DENSITY_HALF * size)
    )


def coupling_kernel(kron_ref, scale_ref, x_ref, out_ref):
    product = jnp.dot(kron_ref[...], x_ref[...], preferred_element_type=F32)
    out_ref[...] = to_i16((product - scale_ref[:, 0:1]) * scale_ref[:, 1:2])


def rows_of_step(wide, step, blocks):
    first = step * blocks * HALO
    return jnp.concatenate(
        [wide[first + k * HALO : first + (k + 1) * HALO] for k in range(blocks)], axis=1
    )


def is_even():
    return (lax.axis_index("tile") & 1) == 0


def pack_kernel(blocks, steps, c_ref, terminal_ref, first_ref, second_ref):
    wide = c_ref[...].astype(F32)
    c = [rows_of_step(wide, t, blocks) for t in range(steps)]
    row = lax.broadcasted_iota(jnp.int32, c[0].shape, 0)
    down = []
    up = []
    for t in range(1, HALO // 2):
        down.append(jnp.where(row >= t, c[HALO - t], pltpu.roll(c[t], t, 0)))
        up.append(jnp.where(row < HALO - t, c[HALO - t], pltpu.roll(c[t], HALO - t, 0)))
    even = is_even()
    edge = terminal_ref[...] * TERMINAL_SCALE
    half = edge.shape[1] // 2
    left, right = c[HALO // 2][:, :half], pltpu.roll(c[HALO // 2][:, half:], HALO // 2, 0)
    upper = row[:, :half] < HALO // 2
    down_mid = jnp.where(upper, right, left)
    up_mid = jnp.where(upper, left, right)

    def stacked(tiles, mid):
        parts = [x[:, at : at + half] for x in tiles + [edge] for at in (0, half)]
        return to_i16(jnp.concatenate(parts + [mid], axis=0))

    first = [jnp.where(even, d, u) for d, u in zip(down, up)]
    second = [jnp.where(even, u, d) for d, u in zip(down, up)]
    first_ref[...] = stacked(first, jnp.where(even, down_mid, up_mid))
    second_ref[...] = stacked(second, jnp.where(even, up_mid, down_mid))


def shares(ahead):
    falling = jnp.minimum(ahead, 0.0)
    low = (time_step * viscosity) * ahead - falling * falling
    return low, ahead * ahead + low


def flux(drift, m, beyond):
    return (jnp.maximum(drift, 0.0) + KAPPA * viscosity) * (m - beyond) + drift * beyond


def backward_kernel(
    blocks, steps, w_ref, c_ref, terminal_ref, init_ref, first_ref, second_ref, u_ref, first_edge_ref, second_edge_ref, sums_ref
):
    pops = w_ref.shape[0]
    cols = terminal_ref.shape[1]
    own = lax.axis_index(POP)
    own_weights = w_ref[pl.ds(own, 1), :].astype(F32)
    total = jnp.sum(own_weights, axis=1, keepdims=True)
    size = jnp.maximum(jnp.sum(jnp.abs(own_weights), axis=1, keepdims=True), 1.0)
    slope = size * (KAPPA * time_step * DENSITY_HALF / (LEVELS * pops))
    offset = total * (KAPPA * time_step * DENSITY_MID / pops)
    wide = c_ref[...].astype(F32)
    even = is_even()
    first = first_ref[...].astype(F32)
    second = second_ref[...].astype(F32)
    above = jnp.where(even, second, first)
    below = jnp.where(even, first, second)

    def tile(x, k):
        at = 2 * k * HALO
        return jnp.concatenate([x[at : at + HALO], x[at + HALO : at + 2 * HALO]], axis=1)

    def middle(x):
        shared = x[HALO * HALO :]
        return jnp.concatenate([shared, pltpu.roll(shared, HALO // 2, 0)], axis=1)

    def levels(t):
        if t == 0:
            top = bottom = jnp.zeros((HALO, cols), F32)
        elif t < HALO // 2:
            top = pltpu.roll(tile(above, t - 1), HALO - t, 0)
            bottom = pltpu.roll(tile(below, t - 1), t, 0)
        elif t == HALO // 2:
            top = middle(above)
            bottom = middle(below)
        else:
            top = tile(above, HALO - t - 1)
            bottom = tile(below, HALO - t - 1)
        return jnp.concatenate([top, rows_of_step(wide, t, blocks), bottom], axis=0)

    last = HALO // 2 - 1
    u = jnp.concatenate(
        [
            tile(above, last) * (KAPPA / TERMINAL_SCALE),
            terminal_ref[...] * KAPPA,
            tile(below, last) * (KAPPA / TERMINAL_SCALE),
        ],
        axis=0,
    )
    high = u.shape[0]
    partial = [None] * steps
    kept = [None] * steps
    for t in reversed(range(steps)):
        ahead_r = pltpu.roll(u, high - 1, 0) - u
        ahead_c = pltpu.roll(u, cols - 1, 1) - u
        low_r, up_r = shares(ahead_r)
        low_c, up_c = shares(ahead_c)
        source = levels(t) * slope + offset
        u = (u + source) + (low_r - pltpu.roll(up_r, 1, 0)) + (low_c - pltpu.roll(up_c, 1, 1))
        u_ref[t] = u
        mine = u[HALO : 2 * HALO]
        kept[t] = mine
        lanes = mine[:, :128]
        for k in range(1, cols // 128):
            lanes = lanes + mine[:, k * 128 : (k + 1) * 128]
        partial[t] = jnp.sum(lanes, axis=0, keepdims=True)
    sums = jnp.sum(jnp.concatenate(partial, axis=0), axis=1, keepdims=True)
    lane = lax.broadcasted_iota(jnp.int32, (steps, 128), 1)
    step = lax.broadcasted_iota(jnp.int32, (steps, 128), 0)
    line = jnp.sum(jnp.where(lane == step, sums, 0.0), axis=0, keepdims=True)
    sums_ref[...] = jnp.broadcast_to(
        jnp.concatenate([line] * (sums_ref.shape[2] // 128), axis=1)[None], sums_ref.shape
    )
    row = lax.broadcasted_iota(jnp.int32, (HALO, cols), 0)
    largest = jnp.maximum(
        jnp.maximum(jnp.abs(kept[0]), jnp.abs(kept[1])),
        jnp.maximum(jnp.abs(kept[2]), jnp.abs(kept[3])),
    )
    largest = jnp.max(jnp.max(largest, axis=1, keepdims=True), axis=0, keepdims=True)
    exponent = jnp.ceil(jnp.log2(jnp.maximum(largest, 1e-30)))
    scale = LEVELS / jnp.exp2(exponent)
    inner = jnp.where((row >= 1) & (row <= 6), kept[1], pltpu.roll(kept[3], 4, 0))
    edges = to_i16(
        jnp.concatenate(
            [
                (init_ref[...] - INIT_MID) * INIT_SCALE,
                kept[0] * scale,
                inner * scale,
                jnp.where(row == 0, exponent, kept[2] * scale),
            ],
            axis=0,
        )
    )
    second_edge_ref[...] = edges
    spare = first_edge_ref.shape[0] - edges.shape[0]
    first_edge_ref[...] = jnp.concatenate([edges, edges[:spare]], axis=0)


def decoded(edge):
    edge = edge.astype(F32)
    size = jnp.exp2(edge[24:25, 0:1]) * (1.0 / LEVELS)
    return jnp.concatenate([edge[0:8] * (1.0 / INIT_SCALE) + INIT_MID, edge[8:32] * size], axis=0)


def forward_kernel(
    cells, steps, u_ref, init_ref, second_ref, first_ref, sums_ref, values_ref, final_ref
):
    cols = init_ref.shape[1]
    row = lax.broadcasted_iota(jnp.int32, (HALO, cols), 0)
    even = is_even()
    first = decoded(first_ref[...])
    second = decoded(second_ref[...])
    above = jnp.where(even, second, first)
    below = jnp.where(even, first, second)
    m = jnp.concatenate([above[0:8], init_ref[...], below[0:8]], axis=0)
    high = m.shape[0]

    def field(t):
        u = u_ref[t]
        if t > 3:
            return u

        def side(far, near):
            if t == 0:
                return far[8:16]
            if t == 1:
                return jnp.where((row >= 1) & (row <= 6), far[16:24], near)
            if t == 2:
                return jnp.where((row >= 2) & (row <= 5), far[24:32], near)
            return jnp.where((row >= 3) & (row <= 4), pltpu.roll(far[16:24], 4, 0), near)

        return jnp.concatenate(
            [side(above, u[0:8]), u[8:16], side(below, u[16:24])], axis=0
        )

    means = jnp.sum(sums_ref[:, :, 0:128], axis=0) * (1.0 / cells)
    for t in range(steps):
        values_ref[t] = (u_ref[t, HALO : 2 * HALO, :] - means[:, t : t + 1]) * (1.0 / KAPPA)
        u = field(t)
        down_m = pltpu.roll(m, high - 1, 0)
        right_m = pltpu.roll(m, cols - 1, 1)
        flux_r = flux(u - pltpu.roll(u, high - 1, 0), m, down_m)
        flux_c = flux(u - pltpu.roll(u, cols - 1, 1), m, right_m)
        m = m - (time_step / KAPPA) * (
            (flux_r - pltpu.roll(flux_r, 1, 0)) + (flux_c - pltpu.roll(flux_c, 1, 1))
        )
    final_ref[...] = m[HALO : 2 * HALO]


def call(kernel, outs, *args):
    spec = pl.BlockSpec(memory_space=pltpu.VMEM)
    return pl.pallas_call(
        kernel,
        out_shape=outs,
        in_specs=[spec] * len(args),
        out_specs=jax.tree.map(lambda _: spec, outs),
        compiler_params=pltpu.CompilerParams(vmem_limit_bytes=40 * 1024 * 1024),
    )(*args)


def first_swap(x):
    peers = lax.axis_size("tile")
    return lax.ppermute(x, "tile", [(i, i ^ 1) for i in range(peers)])


def second_swap(x):
    peers = lax.axis_size("tile")
    return lax.ppermute(x, "tile", [(i, (((i + 1) ^ 1) - 1) % peers) for i in range(peers)])


def per_device(weights, terminal, density_history, density_init):
    pops = weights.shape[0]
    steps, rows, cols = density_history.shape[1:]
    tiles = lax.axis_size("tile")
    blocks = pops // steps
    part = cols // blocks
    struct = jax.ShapeDtypeStruct
    terminal = terminal[0]
    init = density_init[0]
    chunks = density_history[0].reshape(steps, rows, blocks, part).transpose(0, 2, 1, 3)
    chunks = lax.all_to_all(chunks.reshape(pops, rows, part), POP, 0, 0, tiled=True)
    kron, scale = call(
        spread_kernel,
        (struct((pops * rows, pops * rows), jnp.bfloat16), struct((pops * rows, 128), F32)),
        weights,
    )
    levels = call(
        coupling_kernel,
        struct((pops * rows, part), I16),
        kron,
        scale,
        chunks.reshape(pops * rows, part),
    )
    levels = lax.all_to_all(levels.reshape(pops, rows, part), POP, 0, 0, tiled=True)
    levels = levels.reshape(pops * rows, part)
    first, second = call(
        functools.partial(pack_kernel, blocks, steps),
        (struct((72, cols // 2), I16), struct((72, cols // 2), I16)),
        levels,
        terminal,
    )
    second = second_swap(second)
    first = first_swap(first)
    fields, first, second, sums = call(
        functools.partial(backward_kernel, blocks, steps),
        (
            struct((steps, 3 * HALO, cols), F32),
            struct((40, cols), I16),
            struct((32, cols), I16),
            struct((tiles, 1, 1152), F32),
        ),
        weights,
        levels,
        terminal,
        init,
        first,
        second,
    )
    first = first_swap(first)
    second = second_swap(second)
    sums = lax.all_to_all(sums, "tile", 0, 0, tiled=True)
    values, final = call(
        functools.partial(forward_kernel, float(tiles * rows * cols), steps),
        (struct((steps, rows, cols), F32), struct((rows, cols), F32)),
        fields,
        init,
        second,
        first,
        sums,
    )
    return values[None], final[None]


def solution(mesh):
    split = Mesh(
        mesh.devices.reshape(8, 2, 2, mesh.shape["tile"]), ("pop_0", "pop_1", "pop_2", "tile")
    )
    in_specs = (P(), P(POP, "tile", None), P(POP, None, "tile", None), P(POP, "tile", None))
    out_specs = (P(POP, None, "tile", None), P(POP, "tile", None))
    return jax.shard_map(
        per_device, mesh=split, in_specs=in_specs, out_specs=out_specs, check_vma=False
    )
```

```python
import functools

import jax
import jax.numpy as jnp
from jax import lax
from jax.experimental import pallas as pl
from jax.experimental.pallas import tpu as pltpu
from jax.sharding import Mesh
from jax.sharding import PartitionSpec as P

POP = ("pop_0", "pop_1", "pop_2")

time_step = 0.2
viscosity = 0.2

DENSITY_MID = (0.19921875 + 2.0) / 2
DENSITY_HALF = (2.0 - 0.19921875) / 2
LEVELS = 32000.0
TERMINAL_SCALE = 32000.0 / 4.5
INIT_MID = 1.1
INIT_SCALE = 32000.0 / 0.9

HALO = 8
KAPPA = time_step / 2

F32 = jnp.float32
I16 = jnp.int16


def to_i16(x):
    return jnp.round(x).astype(jnp.int32).astype(I16)


def spread_kernel(w_ref, kron_ref, scale_ref):
    pops = w_ref.shape[0]
    rows = kron_ref.shape[0]
    per = rows // pops
    shift = per.bit_length() - 1
    weights = w_ref[...].astype(F32).astype(jnp.bfloat16)
    i = lax.broadcasted_iota(jnp.int32, (rows, pops), 0)
    q = lax.broadcasted_iota(jnp.int32, (rows, pops), 1)
    spread = jnp.where((i >> shift) == q, 1.0, 0.0).astype(jnp.bfloat16)
    tall = jnp.dot(spread, weights, preferred_element_type=F32)
    total = jnp.sum(tall, axis=1, keepdims=True)
    size = jnp.maximum(jnp.sum(jnp.abs(tall), axis=1, keepdims=True), 1.0)
    wide = lax.dot_general(
        tall.astype(jnp.bfloat16), spread, (((1,), (1,)), ((), ())), preferred_element_type=F32
    )
    a = lax.broadcasted_iota(jnp.int32, (rows, rows), 0)
    b = lax.broadcasted_iota(jnp.int32, (rows, rows), 1)
    kron_ref[...] = jnp.where((a & (per - 1)) == (b & (per - 1)), wide, 0.0).astype(jnp.bfloat16)
    lane = lax.broadcasted_iota(jnp.int32, scale_ref.shape, 1)
    scale_ref[...] = jnp.where(
        lane == 0, DENSITY_MID * total, LEVELS / (DENSITY_HALF * size)
    )


def coupling_kernel(kron_ref, scale_ref, x_ref, out_ref):
    product = jnp.dot(kron_ref[...], x_ref[...], preferred_element_type=F32)
    out_ref[...] = to_i16((product - scale_ref[:, 0:1]) * scale_ref[:, 1:2])


def rows_of_step(wide, step, blocks):
    first = step * blocks * HALO
    return jnp.concatenate(
        [wide[first + k * HALO : first + (k + 1) * HALO] for k in range(blocks)], axis=1
    )


def is_even():
    return (lax.axis_index("tile") & 1) == 0


def pack_kernel(blocks, steps, c_ref, terminal_ref, first_ref, second_ref):
    wide = c_ref[...].astype(F32)
    c = [rows_of_step(wide, t, blocks) for t in range(steps)]
    row = lax.broadcasted_iota(jnp.int32, c[0].shape, 0)
    down = []
    up = []
    for t in range(1, HALO // 2):
        down.append(jnp.where(row >= t, c[HALO - t], pltpu.roll(c[t], t, 0)))
        up.append(jnp.where(row < HALO - t, c[HALO - t], pltpu.roll(c[t], HALO - t, 0)))
    even = is_even()
    edge = terminal_ref[...] * TERMINAL_SCALE
    half = edge.shape[1] // 2
    left, right = c[HALO // 2][:, :half], pltpu.roll(c[HALO // 2][:, half:], HALO // 2, 0)
    upper = row[:, :half] < HALO // 2
    down_mid = jnp.where(upper, right, left)
    up_mid = jnp.where(upper, left, right)

    def stacked(tiles, mid):
        parts = [x[:, at : at + half] for x in tiles + [edge] for at in (0, half)]
        return to_i16(jnp.concatenate(parts + [mid], axis=0))

    first = [jnp.where(even, d, u) for d, u in zip(down, up)]
    second = [jnp.where(even, u, d) for d, u in zip(down, up)]
    first_ref[...] = stacked(first, jnp.where(even, down_mid, up_mid))
    second_ref[...] = stacked(second, jnp.where(even, up_mid, down_mid))


def shares(ahead):
    falling = jnp.minimum(ahead, 0.0)
    low = (time_step * viscosity) * ahead - falling * falling
    return low, ahead * ahead + low


def flux(drift, m, beyond):
    return (jnp.maximum(drift, 0.0) + KAPPA * viscosity) * (m - beyond) + drift * beyond


def backward_kernel(
    blocks, steps, w_ref, c_ref, terminal_ref, init_ref, first_ref, second_ref, u_ref, first_edge_ref, second_edge_ref, sums_ref
):
    pops = w_ref.shape[0]
    cols = terminal_ref.shape[1]
    own = lax.axis_index(POP)
    own_weights = w_ref[pl.ds(own, 1), :].astype(F32)
    total = jnp.sum(own_weights, axis=1, keepdims=True)
    size = jnp.maximum(jnp.sum(jnp.abs(own_weights), axis=1, keepdims=True), 1.0)
    slope = size * (KAPPA * time_step * DENSITY_HALF / (LEVELS * pops))
    offset = total * (KAPPA * time_step * DENSITY_MID / pops)
    wide = c_ref[...].astype(F32)
    even = is_even()
    first = first_ref[...].astype(F32)
    second = second_ref[...].astype(F32)
    above = jnp.where(even, second, first)
    below = jnp.where(even, first, second)

    def tile(x, k):
        at = 2 * k * HALO
        return jnp.concatenate([x[at : at + HALO], x[at + HALO : at + 2 * HALO]], axis=1)

    def middle(x):
        shared = x[HALO * HALO :]
        return jnp.concatenate([shared, pltpu.roll(shared, HALO // 2, 0)], axis=1)

    def levels(t):
        if t == 0:
            top = bottom = jnp.zeros((HALO, cols), F32)
        elif t < HALO // 2:
            top = pltpu.roll(tile(above, t - 1), HALO - t, 0)
            bottom = pltpu.roll(tile(below, t - 1), t, 0)
        elif t == HALO // 2:
            top = middle(above)
            bottom = middle(below)
        else:
            top = tile(above, HALO - t - 1)
            bottom = tile(below, HALO - t - 1)
        return jnp.concatenate([top, rows_of_step(wide, t, blocks), bottom], axis=0)

    last = HALO // 2 - 1
    u = jnp.concatenate(
        [
            tile(above, last) * (KAPPA / TERMINAL_SCALE),
            terminal_ref[...] * KAPPA,
            tile(below, last) * (KAPPA / TERMINAL_SCALE),
        ],
        axis=0,
    )
    high = u.shape[0]
    partial = [None] * steps
    kept = [None] * steps
    for t in reversed(range(steps)):
        ahead_r = pltpu.roll(u, high - 1, 0) - u
        ahead_c = pltpu.roll(u, cols - 1, 1) - u
        low_r, up_r = shares(ahead_r)
        low_c, up_c = shares(ahead_c)
        source = levels(t) * slope + offset
        u = (u + source) + (low_r - pltpu.roll(up_r, 1, 0)) + (low_c - pltpu.roll(up_c, 1, 1))
        mine = u[HALO : 2 * HALO]
        if t == 0:
            u_ref[t, HALO : 2 * HALO, :] = mine
        else:
            u_ref[t] = u
        kept[t] = mine
        lanes = mine[:, :128]
        for k in range(1, cols // 128):
            lanes = lanes + mine[:, k * 128 : (k + 1) * 128]
        partial[t] = jnp.sum(lanes, axis=0, keepdims=True)
    sums = jnp.sum(jnp.concatenate(partial, axis=0), axis=1, keepdims=True)
    lane = lax.broadcasted_iota(jnp.int32, (steps, 128), 1)
    step = lax.broadcasted_iota(jnp.int32, (steps, 128), 0)
    line = jnp.sum(jnp.where(lane == step, sums, 0.0), axis=0, keepdims=True)
    sums_ref[...] = jnp.broadcast_to(
        jnp.concatenate([line] * (sums_ref.shape[2] // 128), axis=1)[None], sums_ref.shape
    )
    row = lax.broadcasted_iota(jnp.int32, (HALO, cols), 0)
    largest = jnp.maximum(
        jnp.maximum(jnp.abs(kept[0]), jnp.abs(kept[1])),
        jnp.maximum(jnp.abs(kept[2]), jnp.abs(kept[3])),
    )
    largest = jnp.max(jnp.max(largest, axis=1, keepdims=True), axis=0, keepdims=True)
    exponent = jnp.ceil(jnp.log2(jnp.maximum(largest, 1e-30)))
    scale = LEVELS / jnp.exp2(exponent)
    inner = jnp.where((row >= 1) & (row <= 6), kept[1], pltpu.roll(kept[3], 4, 0))
    edges = to_i16(
        jnp.concatenate(
            [
                (init_ref[...] - INIT_MID) * INIT_SCALE,
                kept[0] * scale,
                inner * scale,
                jnp.where(row == 0, exponent, kept[2] * scale),
            ],
            axis=0,
        )
    )
    second_edge_ref[...] = edges
    spare = first_edge_ref.shape[0] - edges.shape[0]
    first_edge_ref[...] = jnp.concatenate([edges, edges[:spare]], axis=0)


def decoded(edge):
    edge = edge.astype(F32)
    size = jnp.exp2(edge[24:25, 0:1]) * (1.0 / LEVELS)
    return jnp.concatenate([edge[0:8] * (1.0 / INIT_SCALE) + INIT_MID, edge[8:32] * size], axis=0)


def forward_kernel(
    cells, steps, u_ref, init_ref, second_ref, first_ref, sums_ref, values_ref, final_ref
):
    cols = init_ref.shape[1]
    row = lax.broadcasted_iota(jnp.int32, (HALO, cols), 0)
    even = is_even()
    first = decoded(first_ref[...])
    second = decoded(second_ref[...])
    above = jnp.where(even, second, first)
    below = jnp.where(even, first, second)
    m = jnp.concatenate([above[0:8], init_ref[...], below[0:8]], axis=0)
    high = m.shape[0]

    def field(t):
        if t == 0:
            own = u_ref[0, HALO : 2 * HALO, :]
            return jnp.concatenate([above[8:16], own, below[8:16]], axis=0)
        u = u_ref[t]
        if t > 3:
            return u

        def side(far, near):
            if t == 1:
                return jnp.where((row >= 1) & (row <= 6), far[16:24], near)
            if t == 2:
                return jnp.where((row >= 2) & (row <= 5), far[24:32], near)
            return jnp.where((row >= 3) & (row <= 4), pltpu.roll(far[16:24], 4, 0), near)

        return jnp.concatenate(
            [side(above, u[0:8]), u[8:16], side(below, u[16:24])], axis=0
        )

    means = jnp.sum(sums_ref[:, :, 0:128], axis=0) * (1.0 / cells)
    for t in range(steps):
        values_ref[t] = (u_ref[t, HALO : 2 * HALO, :] - means[:, t : t + 1]) * (1.0 / KAPPA)
        u = field(t)
        down_m = pltpu.roll(m, high - 1, 0)
        right_m = pltpu.roll(m, cols - 1, 1)
        flux_r = flux(u - pltpu.roll(u, high - 1, 0), m, down_m)
        flux_c = flux(u - pltpu.roll(u, cols - 1, 1), m, right_m)
        m = m - (time_step / KAPPA) * (
            (flux_r - pltpu.roll(flux_r, 1, 0)) + (flux_c - pltpu.roll(flux_c, 1, 1))
        )
    final_ref[...] = m[HALO : 2 * HALO]


def call(kernel, outs, *args):
    spec = pl.BlockSpec(memory_space=pltpu.VMEM)
    return pl.pallas_call(
        kernel,
        out_shape=outs,
        in_specs=[spec] * len(args),
        out_specs=jax.tree.map(lambda _: spec, outs),
        compiler_params=pltpu.CompilerParams(vmem_limit_bytes=40 * 1024 * 1024),
    )(*args)


def first_swap(x):
    peers = lax.axis_size("tile")
    return lax.ppermute(x, "tile", [(i, i ^ 1) for i in range(peers)])


def second_swap(x):
    peers = lax.axis_size("tile")
    return lax.ppermute(x, "tile", [(i, (((i + 1) ^ 1) - 1) % peers) for i in range(peers)])


def per_device(weights, terminal, density_history, density_init):
    pops = weights.shape[0]
    steps, rows, cols = density_history.shape[1:]
    tiles = lax.axis_size("tile")
    blocks = pops // steps
    part = cols // blocks
    struct = jax.ShapeDtypeStruct
    terminal = terminal[0]
    init = density_init[0]
    chunks = density_history[0].reshape(steps, rows, blocks, part).transpose(0, 2, 1, 3)
    chunks = lax.all_to_all(chunks.reshape(pops, rows, part), POP, 0, 0, tiled=True)
    kron, scale = call(
        spread_kernel,
        (struct((pops * rows, pops * rows), jnp.bfloat16), struct((pops * rows, 128), F32)),
        weights,
    )
    levels = call(
        coupling_kernel,
        struct((pops * rows, part), I16),
        kron,
        scale,
        chunks.reshape(pops * rows, part),
    )
    levels = lax.all_to_all(levels.reshape(pops, rows, part), POP, 0, 0, tiled=True)
    levels = levels.reshape(pops * rows, part)
    first, second = call(
        functools.partial(pack_kernel, blocks, steps),
        (struct((72, cols // 2), I16), struct((72, cols // 2), I16)),
        levels,
        terminal,
    )
    second = second_swap(second)
    first = first_swap(first)
    fields, first, second, sums = call(
        functools.partial(backward_kernel, blocks, steps),
        (
            struct((steps, 3 * HALO, cols), F32),
            struct((40, cols), I16),
            struct((32, cols), I16),
            struct((tiles, 1, 1152), F32),
        ),
        weights,
        levels,
        terminal,
        init,
        first,
        second,
    )
    first = first_swap(first)
    second = second_swap(second)
    sums = lax.all_to_all(sums, "tile", 0, 0, tiled=True)
    values, final = call(
        functools.partial(forward_kernel, float(tiles * rows * cols), steps),
        (struct((steps, rows, cols), F32), struct((rows, cols), F32)),
        fields,
        init,
        second,
        first,
        sums,
    )
    return values[None], final[None]


def solution(mesh):
    split = Mesh(
        mesh.devices.reshape(8, 2, 2, mesh.shape["tile"]), ("pop_0", "pop_1", "pop_2", "tile")
    )
    in_specs = (P(), P(POP, "tile", None), P(POP, None, "tile", None), P(POP, "tile", None))
    out_specs = (P(POP, None, "tile", None), P(POP, "tile", None))
    return jax.shard_map(
        per_device, mesh=split, in_specs=in_specs, out_specs=out_specs, check_vma=False
    )
```

```python
import functools

import jax
import jax.numpy as jnp
from jax import lax
from jax.experimental import pallas as pl
from jax.experimental.pallas import tpu as pltpu
from jax.sharding import Mesh
from jax.sharding import PartitionSpec as P

POP = ("pop_0", "pop_1", "pop_2")

time_step = 0.2
viscosity = 0.2

DENSITY_MID = (0.19921875 + 2.0) / 2
DENSITY_HALF = (2.0 - 0.19921875) / 2
LEVELS = 32000.0
TERMINAL_SCALE = 32000.0 / 4.5
INIT_MID = 1.1
INIT_SCALE = 32000.0 / 0.9

HALO = 8
KAPPA = time_step / 2

F32 = jnp.float32
I16 = jnp.int16


def to_i16(x):
    return jnp.round(x).astype(jnp.int32).astype(I16)


def spread_kernel(w_ref, kron_ref, scale_ref):
    pops = w_ref.shape[0]
    rows = kron_ref.shape[0]
    per = rows // pops
    shift = per.bit_length() - 1
    weights = w_ref[...].astype(F32).astype(jnp.bfloat16)
    i = lax.broadcasted_iota(jnp.int32, (rows, pops), 0)
    q = lax.broadcasted_iota(jnp.int32, (rows, pops), 1)
    spread = jnp.where((i >> shift) == q, 1.0, 0.0).astype(jnp.bfloat16)
    tall = jnp.dot(spread, weights, preferred_element_type=F32)
    total = jnp.sum(tall, axis=1, keepdims=True)
    size = jnp.maximum(jnp.sum(jnp.abs(tall), axis=1, keepdims=True), 1.0)
    wide = lax.dot_general(
        tall.astype(jnp.bfloat16), spread, (((1,), (1,)), ((), ())), preferred_element_type=F32
    )
    a = lax.broadcasted_iota(jnp.int32, (rows, rows), 0)
    b = lax.broadcasted_iota(jnp.int32, (rows, rows), 1)
    kron_ref[...] = jnp.where((a & (per - 1)) == (b & (per - 1)), wide, 0.0).astype(jnp.bfloat16)
    lane = lax.broadcasted_iota(jnp.int32, scale_ref.shape, 1)
    scale_ref[...] = jnp.where(
        lane == 0, DENSITY_MID * total, LEVELS / (DENSITY_HALF * size)
    )


def coupling_kernel(kron_ref, scale_ref, x_ref, out_ref):
    product = jnp.dot(kron_ref[...], x_ref[...], preferred_element_type=F32)
    out_ref[...] = to_i16((product - scale_ref[:, 0:1]) * scale_ref[:, 1:2])


def rows_of_step(wide, step, blocks):
    first = step * blocks * HALO
    return jnp.concatenate(
        [wide[first + k * HALO : first + (k + 1) * HALO] for k in range(blocks)], axis=1
    )


def is_even():
    return (lax.axis_index("tile") & 1) == 0


def pack_kernel(blocks, steps, c_ref, terminal_ref, first_ref, second_ref):
    wide = c_ref[...].astype(F32)
    c = [rows_of_step(wide, t, blocks) for t in range(steps)]
    row = lax.broadcasted_iota(jnp.int32, c[0].shape, 0)
    down = []
    up = []
    for t in range(1, HALO // 2):
        down.append(jnp.where(row >= t, c[HALO - t], pltpu.roll(c[t], t, 0)))
        up.append(jnp.where(row < HALO - t, c[HALO - t], pltpu.roll(c[t], HALO - t, 0)))
    even = is_even()
    edge = terminal_ref[...] * TERMINAL_SCALE
    half = edge.shape[1] // 2
    left, right = c[HALO // 2][:, :half], pltpu.roll(c[HALO // 2][:, half:], HALO // 2, 0)
    upper = row[:, :half] < HALO // 2
    down_mid = jnp.where(upper, right, left)
    up_mid = jnp.where(upper, left, right)

    def stacked(tiles, mid):
        parts = [x[:, at : at + half] for x in tiles + [edge] for at in (0, half)]
        return to_i16(jnp.concatenate(parts + [mid], axis=0))

    first = [jnp.where(even, d, u) for d, u in zip(down, up)]
    second = [jnp.where(even, u, d) for d, u in zip(down, up)]
    first_ref[...] = stacked(first, jnp.where(even, down_mid, up_mid))
    second_ref[...] = stacked(second, jnp.where(even, up_mid, down_mid))


def shares(ahead):
    falling = jnp.minimum(ahead, 0.0)
    low = (time_step * viscosity) * ahead - falling * falling
    return low, ahead * ahead + low


def flux(drift, m, beyond):
    return (jnp.maximum(drift, 0.0) + KAPPA * viscosity) * (m - beyond) + drift * beyond


def backward_kernel(
    blocks, steps, w_ref, c_ref, terminal_ref, init_ref, first_ref, second_ref, u_ref, first_edge_ref, second_edge_ref, sums_ref
):
    pops = w_ref.shape[0]
    cols = terminal_ref.shape[1]
    own = lax.axis_index(POP)
    own_weights = w_ref[pl.ds(own, 1), :].astype(F32)
    total = jnp.sum(own_weights, axis=1, keepdims=True)
    size = jnp.maximum(jnp.sum(jnp.abs(own_weights), axis=1, keepdims=True), 1.0)
    slope = size * (KAPPA * time_step * DENSITY_HALF / (LEVELS * pops))
    offset = total * (KAPPA * time_step * DENSITY_MID / pops)
    wide = c_ref[...].astype(F32)
    even = is_even()
    first = first_ref[...].astype(F32)
    second = second_ref[...].astype(F32)
    above = jnp.where(even, second, first)
    below = jnp.where(even, first, second)

    def tile(x, k):
        at = 2 * k * HALO
        return jnp.concatenate([x[at : at + HALO], x[at + HALO : at + 2 * HALO]], axis=1)

    def middle(x):
        shared = x[HALO * HALO :]
        return jnp.concatenate([shared, pltpu.roll(shared, HALO // 2, 0)], axis=1)

    def levels(t):
        if t == 0:
            top = bottom = jnp.zeros((HALO, cols), F32)
        elif t < HALO // 2:
            top = pltpu.roll(tile(above, t - 1), HALO - t, 0)
            bottom = pltpu.roll(tile(below, t - 1), t, 0)
        elif t == HALO // 2:
            top = middle(above)
            bottom = middle(below)
        else:
            top = tile(above, HALO - t - 1)
            bottom = tile(below, HALO - t - 1)
        return jnp.concatenate([top, rows_of_step(wide, t, blocks), bottom], axis=0)

    last = HALO // 2 - 1
    u = jnp.concatenate(
        [
            tile(above, last) * (KAPPA / TERMINAL_SCALE),
            terminal_ref[...] * KAPPA,
            tile(below, last) * (KAPPA / TERMINAL_SCALE),
        ],
        axis=0,
    )
    high = u.shape[0]
    partial = [None] * steps
    kept = [None] * steps
    for t in reversed(range(steps)):
        ahead_r = pltpu.roll(u, high - 1, 0) - u
        ahead_c = pltpu.roll(u, cols - 1, 1) - u
        low_r, up_r = shares(ahead_r)
        low_c, up_c = shares(ahead_c)
        source = levels(t) * slope + offset
        u = (u + source) + (low_r - pltpu.roll(up_r, 1, 0)) + (low_c - pltpu.roll(up_c, 1, 1))
        mine = u[HALO : 2 * HALO]
        if t == 0:
            u_ref[t, HALO : 2 * HALO, :] = mine
        else:
            u_ref[t] = u
        kept[t] = mine
        lanes = mine[:, :128]
        for k in range(1, cols // 128):
            lanes = lanes + mine[:, k * 128 : (k + 1) * 128]
        partial[t] = jnp.sum(lanes, axis=0, keepdims=True)
    sums = jnp.sum(jnp.concatenate(partial, axis=0), axis=1, keepdims=True)
    lane = lax.broadcasted_iota(jnp.int32, (steps, 128), 1)
    step = lax.broadcasted_iota(jnp.int32, (steps, 128), 0)
    line = jnp.sum(jnp.where(lane == step, sums, 0.0), axis=0, keepdims=True)
    sums_ref[...] = jnp.broadcast_to(
        jnp.concatenate([line] * (sums_ref.shape[2] // 128), axis=1)[None], sums_ref.shape
    )
    row = lax.broadcasted_iota(jnp.int32, (HALO, cols), 0)
    largest = jnp.maximum(
        jnp.maximum(jnp.abs(kept[0]), jnp.abs(kept[1])),
        jnp.maximum(jnp.abs(kept[2]), jnp.abs(kept[3])),
    )
    largest = jnp.max(jnp.max(largest, axis=1, keepdims=True), axis=0, keepdims=True)
    exponent = jnp.ceil(jnp.log2(jnp.maximum(largest, 1e-30)))
    scale = LEVELS / jnp.exp2(exponent)
    inner = jnp.where((row >= 1) & (row <= 6), kept[1], pltpu.roll(kept[3], 4, 0))
    edges = [
        (init_ref[...] - INIT_MID) * INIT_SCALE,
        kept[0] * scale,
        inner * scale,
        jnp.where(row == 0, exponent, kept[2] * scale),
    ]
    second_edge_ref[...] = to_i16(jnp.concatenate(edges, axis=0))
    first_edge_ref[...] = to_i16(jnp.concatenate(edges + edges[:1], axis=0))


def decoded(edge):
    edge = edge.astype(F32)
    size = jnp.exp2(edge[24:25, 0:1]) * (1.0 / LEVELS)
    return jnp.concatenate([edge[0:8] * (1.0 / INIT_SCALE) + INIT_MID, edge[8:32] * size], axis=0)


def forward_kernel(
    cells, steps, u_ref, init_ref, second_ref, first_ref, sums_ref, values_ref, final_ref
):
    cols = init_ref.shape[1]
    row = lax.broadcasted_iota(jnp.int32, (HALO, cols), 0)
    even = is_even()
    first = decoded(first_ref[...])
    second = decoded(second_ref[...])
    above = jnp.where(even, second, first)
    below = jnp.where(even, first, second)
    m = jnp.concatenate([above[0:8], init_ref[...], below[0:8]], axis=0)
    high = m.shape[0]

    def field(t):
        if t == 0:
            own = u_ref[0, HALO : 2 * HALO, :]
            return jnp.concatenate([above[8:16], own, below[8:16]], axis=0)
        u = u_ref[t]
        if t > 3:
            return u

        def side(far, near):
            if t == 1:
                return jnp.where((row >= 1) & (row <= 6), far[16:24], near)
            if t == 2:
                return jnp.where((row >= 2) & (row <= 5), far[24:32], near)
            return jnp.where((row >= 3) & (row <= 4), pltpu.roll(far[16:24], 4, 0), near)

        return jnp.concatenate(
            [side(above, u[0:8]), u[8:16], side(below, u[16:24])], axis=0
        )

    means = jnp.sum(sums_ref[:, :, 0:128], axis=0) * (1.0 / cells)
    for t in range(steps):
        values_ref[t] = (u_ref[t, HALO : 2 * HALO, :] - means[:, t : t + 1]) * (1.0 / KAPPA)
        u = field(t)
        down_m = pltpu.roll(m, high - 1, 0)
        right_m = pltpu.roll(m, cols - 1, 1)
        flux_r = flux(u - pltpu.roll(u, high - 1, 0), m, down_m)
        flux_c = flux(u - pltpu.roll(u, cols - 1, 1), m, right_m)
        m = m - (time_step / KAPPA) * (
            (flux_r - pltpu.roll(flux_r, 1, 0)) + (flux_c - pltpu.roll(flux_c, 1, 1))
        )
    final_ref[...] = m[HALO : 2 * HALO]


def call(kernel, outs, *args):
    spec = pl.BlockSpec(memory_space=pltpu.VMEM)
    return pl.pallas_call(
        kernel,
        out_shape=outs,
        in_specs=[spec] * len(args),
        out_specs=jax.tree.map(lambda _: spec, outs),
        compiler_params=pltpu.CompilerParams(vmem_limit_bytes=40 * 1024 * 1024),
    )(*args)


def first_swap(x):
    peers = lax.axis_size("tile")
    return lax.ppermute(x, "tile", [(i, i ^ 1) for i in range(peers)])


def second_swap(x):
    peers = lax.axis_size("tile")
    return lax.ppermute(x, "tile", [(i, (((i + 1) ^ 1) - 1) % peers) for i in range(peers)])


def per_device(weights, terminal, density_history, density_init):
    pops = weights.shape[0]
    steps, rows, cols = density_history.shape[1:]
    tiles = lax.axis_size("tile")
    blocks = pops // steps
    part = cols // blocks
    struct = jax.ShapeDtypeStruct
    terminal = terminal[0]
    init = density_init[0]
    chunks = density_history[0].reshape(steps, rows, blocks, part).transpose(0, 2, 1, 3)
    chunks = lax.all_to_all(chunks.reshape(pops, rows, part), POP, 0, 0, tiled=True)
    kron, scale = call(
        spread_kernel,
        (struct((pops * rows, pops * rows), jnp.bfloat16), struct((pops * rows, 128), F32)),
        weights,
    )
    levels = call(
        coupling_kernel,
        struct((pops * rows, part), I16),
        kron,
        scale,
        chunks.reshape(pops * rows, part),
    )
    levels = lax.all_to_all(levels.reshape(pops, rows, part), POP, 0, 0, tiled=True)
    levels = levels.reshape(pops * rows, part)
    first, second = call(
        functools.partial(pack_kernel, blocks, steps),
        (struct((72, cols // 2), I16), struct((72, cols // 2), I16)),
        levels,
        terminal,
    )
    second = second_swap(second)
    first = first_swap(first)
    fields, first, second, sums = call(
        functools.partial(backward_kernel, blocks, steps),
        (
            struct((steps, 3 * HALO, cols), F32),
            struct((40, cols), I16),
            struct((32, cols), I16),
            struct((tiles, 1, 1152), F32),
        ),
        weights,
        levels,
        terminal,
        init,
        first,
        second,
    )
    first = first_swap(first)
    second = second_swap(second)
    sums = lax.all_to_all(sums, "tile", 0, 0, tiled=True)
    values, final = call(
        functools.partial(forward_kernel, float(tiles * rows * cols), steps),
        (struct((steps, rows, cols), F32), struct((rows, cols), F32)),
        fields,
        init,
        second,
        first,
        sums,
    )
    return values[None], final[None]


def solution(mesh):
    split = Mesh(
        mesh.devices.reshape(8, 2, 2, mesh.shape["tile"]), ("pop_0", "pop_1", "pop_2", "tile")
    )
    in_specs = (P(), P(POP, "tile", None), P(POP, None, "tile", None), P(POP, "tile", None))
    out_specs = (P(POP, None, "tile", None), P(POP, "tile", None))
    return jax.shard_map(
        per_device, mesh=split, in_specs=in_specs, out_specs=out_specs, check_vma=False
    )
```
